32 devices in a mesh: seq: 4 (over y, core), head: 8 (over z, x).
Axes of the slice: x: 2, y: 2, z: 4, core: 2. Of those that a mesh axis runs over, the one named last changes fastest.
Arguments:
- out_grad: bfloat16 [8192, 4096], P(('seq', 'head')), may hold values from -6 to 6
- out_weight: bfloat16 [4096, 4096], P('head'), may hold values from -0.09375 to 0.09375
- queries: bfloat16 [8192, 4096], P('seq', 'head'), may hold values from -4 to 4
- key_rows: bfloat16 [8192, 4096], P('seq', 'head'), may hold values from -4 to 4
- value_rows: bfloat16 [8192, 4096], P('seq', 'head')
- gate_out: bfloat16 [8192, 4096], P('seq', 'head'), may hold values from -6 to 6
- doc_starts: int32 [3], replicated, may hold values from 0 to 8191, as said below
Outputs:
- grad_queries: bfloat16 [8192, 4096], P('seq', 'head')
- grad_keys: bfloat16 [8192, 4096], P('seq', 'head')
- grad_values: bfloat16 [8192, 4096], P('seq', 'head')
- grad_gate: bfloat16 [8192, 4096], P('seq', 'head')
The draws below stay inside these ranges and needn't reach their ends.
Inputs may be any that keep to these rules, and one draw needn't show every extreme that they name: `doc_starts`: strictly increasing token offsets; the first is 0 and the last is 8191.
All inputs are finite; a program needn't handle non-finite values.
Results may differ from the reference program's by a relative error of at most 0.0058.
Values may be sent and summed in bfloat16 or wider, within the bound.
No kernel may reach another device: no remote copies, remote signals or barrier semaphores. Data moves between devices by JAX's collectives and lax.ppermute only.
A program may use at most 128 MiB of HBM per device.

```python
import math
import jax
import jax.numpy as jnp
from jax import lax

D = 4096
HEADS = 32
HEAD_DIM = 128
BLK = 512
HDIM = 4096
TOKENS = 8192
DOCS = 3


def draw_value_rows(key, part):
    first_key = jax.random.fold_in(key, 11)
    second_key = jax.random.fold_in(key, 12)
    columns = jnp.arange(HDIM, dtype=jnp.int32)
    head_pos = (columns // HEAD_DIM).astype(jnp.float32) / (HEADS - 1)
    rising = jnp.exp(head_pos * math.log(3.0))
    spread = jnp.exp(jax.random.uniform(second_key, (HDIM,), jnp.float32) * math.log(10.0))
    base = jnp.clip(jax.random.normal(first_key, (TOKENS, HDIM), jnp.float32), -6.0, 6.0)
    values = 0.3 * base * rising[None, :] * spread[None, :]
    return values.astype(jnp.bfloat16)


def draw_doc_starts(key, part):
    picks = jax.random.permutation(jax.random.fold_in(key, 21), TOKENS - 2)[:DOCS - 2] + 1
    ordered = jnp.sort(picks.astype(jnp.int32))
    first = jnp.zeros((1,), jnp.int32)
    last = jnp.full((1,), TOKENS - 1, jnp.int32)
    return jnp.concatenate([first, ordered, last])


def shard_levels(stream_key, shape, cuts, smallest, high):
    gain, own = 1.0, jax.random.fold_in(stream_key, 6)
    for axis_at, shards_of in cuts:
        draws = jnp.exp(jax.random.uniform(jax.random.fold_in(own, axis_at), (shards_of,), jnp.float32, smallest / len(cuts), high / len(cuts)))
        gain = gain * jnp.repeat(draws, shape[axis_at] // shards_of).reshape([-1 if axis == axis_at else 1 for axis in range(len(shape))])
    return gain


def normal_values(key, dims, width, bound, shards=(), kind=jnp.bfloat16):
    result = jax.random.normal(key, dims, jnp.float32) * width
    if len(shards) > 0:
        result = shard_levels(key, dims, shards, -0.22, 0.18) * result
    return jnp.clip(result, min=-bound, max=bound).astype(kind)


def setup_inputs(seed: int = 0) -> dict:
    arg_keys = jax.random.split(jax.random.key(seed), 8)
    out_grad = normal_values(arg_keys[0], (TOKENS, D), 1.0, 6.0, ((0, 32),))
    out_weight = normal_values(arg_keys[1], (HDIM, D), D ** -0.5, 0.09375, ((0, 8),))
    queries = normal_values(arg_keys[2], (TOKENS, HDIM), 0.25, 4.0, ((0, 4), (1, 8)))
    key_rows = normal_values(arg_keys[3], (TOKENS, HDIM), 0.25, 4.0, ((0, 4), (1, 8)))
    value_rows = draw_value_rows(jax.random.fold_in(arg_keys[7], 71), 0)
    gate_out = normal_values(arg_keys[5], (TOKENS, HDIM), 1.0, 6.0, ((0, 4), (1, 8)))
    doc_starts = draw_doc_starts(jax.random.fold_in(arg_keys[7], 71), 0)
    return dict(out_grad=out_grad, out_weight=out_weight, queries=queries, key_rows=key_rows, value_rows=value_rows, gate_out=gate_out, doc_starts=doc_starts)


EPS = 1e-06

def block_masks(doc_block, mark_block):
    first_doc = doc_block[0]
    last_doc = doc_block[-1]
    keep_in = ((doc_block == first_doc) & (mark_block[0] == 0)).astype(jnp.float32)
    keep_out = (doc_block == last_doc).astype(jnp.float32)
    blocked = jnp.where((last_doc != first_doc) | (mark_block[0] == 1), jnp.float32(1.0), jnp.float32(0.0))
    order = jnp.arange(doc_block.shape[0], dtype=jnp.int32)
    causal = (order[None, :] <= order[:, None]) & (doc_block[None, :] == doc_block[:, None])
    return (keep_in, keep_out, blocked, causal.astype(jnp.float32))

def reference(out_grad, out_weight, queries, key_rows, value_rows, gate_out, doc_starts):
    f32 = jnp.float32
    bf16 = jnp.bfloat16
    positions = jnp.arange(TOKENS, dtype=jnp.int32)
    doc_ids = lax.optimization_barrier(jnp.sum((doc_starts[None, :] <= positions[:, None]).astype(jnp.int32), axis=1)) - 1
    marks = lax.optimization_barrier(jnp.sum((doc_starts[None, :] == positions[:, None]).astype(jnp.int32), axis=1))
    grad_mix = jnp.dot(out_grad.astype(f32), out_weight.astype(f32).T, preferred_element_type=f32)
    nblocks = TOKENS // BLK

    def split(array):
        return array.reshape(nblocks, BLK, HEADS, HEAD_DIM)
    query_blocks = split(queries)
    key_blocks = split(key_rows)
    value_blocks = split(value_rows)
    doc_blocks = doc_ids.reshape(nblocks, BLK)
    mark_blocks = marks.reshape(nblocks, BLK)

    def forward_step(state, inputs):
        query_b, key_b, value_b, doc_b, mark_b = inputs
        keep_in, keep_out, blocked, causal = block_masks(doc_b, mark_b)
        scores = jnp.einsum('thd,shd->hts', query_b.astype(f32), key_b.astype(f32))
        probs = (scores * causal[None]).astype(bf16)
        state_low = state.astype(bf16)
        intra = jnp.einsum('hts,she->the', probs.astype(f32), value_b.astype(f32))
        inter = jnp.einsum('thd,hde->the', query_b.astype(f32), state_low.astype(f32)) * keep_in[:, None, None]
        masked_keys = key_b * keep_out.astype(bf16)[:, None, None]
        element = jnp.einsum('shd,she->hde', masked_keys.astype(f32), value_b.astype(f32))
        return (element + (1.0 - blocked) * state, (intra + inter, state_low))
    zero_state = jnp.zeros((HEADS, HEAD_DIM, HEAD_DIM), f32)
    _, (attn_blocks, forward_low) = lax.scan(forward_step, zero_state, (query_blocks, key_blocks, value_blocks, doc_blocks, mark_blocks))
    attn_out = attn_blocks.reshape(TOKENS, HDIM)
    rms = jnp.sqrt(lax.optimization_barrier(jnp.sum(attn_out * attn_out, axis=1)) / HDIM + EPS)
    grad_gate = (grad_mix * attn_out / rms[:, None]).astype(bf16)
    gated = grad_mix * gate_out.astype(f32)
    cross = lax.optimization_barrier(jnp.sum(gated * attn_out, axis=1))
    grad_attn = (gated / rms[:, None] - attn_out * (cross / (HDIM * rms ** 3))[:, None]).astype(bf16)
    grad_blocks = split(grad_attn)

    def backward_step(state, inputs):
        query_b, key_b, value_b, grad_b, doc_b, mark_b, forward_b = inputs
        keep_in, keep_out, blocked, causal = block_masks(doc_b, mark_b)
        scores = jnp.einsum('thd,shd->hts', query_b.astype(f32), key_b.astype(f32))
        probs = (scores * causal[None]).astype(bf16).astype(f32)
        dscore = jnp.einsum('the,she->hts', grad_b.astype(f32), value_b.astype(f32))
        dprob = (dscore * causal[None]).astype(bf16).astype(f32)
        state_low = state.astype(bf16).astype(f32)
        forward_f = forward_b.astype(f32)
        grad_q = jnp.einsum('hts,shd->thd', dprob, key_b.astype(f32))
        grad_q = grad_q + keep_in[:, None, None] * jnp.einsum('the,hde->thd', grad_b.astype(f32), forward_f)
        grad_k = jnp.einsum('hts,thd->shd', dprob, query_b.astype(f32))
        grad_k = grad_k + keep_out[:, None, None] * jnp.einsum('she,hde->shd', value_b.astype(f32), state_low)
        grad_v = jnp.einsum('hts,the->she', probs, grad_b.astype(f32))
        grad_v = grad_v + keep_out[:, None, None] * jnp.einsum('shd,hde->she', key_b.astype(f32), state_low)
        masked_queries = query_b * keep_in.astype(bf16)[:, None, None]
        element = jnp.einsum('thd,the->hde', masked_queries.astype(f32), grad_b.astype(f32))
        outputs = (grad_q.astype(bf16), grad_k.astype(bf16), grad_v.astype(bf16))
        return (element + (1.0 - blocked) * state, outputs)
    _, (grad_q_blocks, grad_k_blocks, grad_v_blocks) = lax.scan(backward_step, zero_state, (query_blocks, key_blocks, value_blocks, grad_blocks, doc_blocks, mark_blocks, forward_low), reverse=True)
    return (grad_q_blocks.reshape(TOKENS, HDIM), grad_k_blocks.reshape(TOKENS, HDIM), grad_v_blocks.reshape(TOKENS, HDIM), grad_gate)
```

```python
import functools

import jax
import jax.numpy as jnp
from jax import lax
from jax.experimental import pallas as pl
from jax.experimental.pallas import tpu as pltpu
from jax.sharding import PartitionSpec as P

HEAD_DIM = 128
BLK = 512
SUB = 256
EPS = 1e-06
F32 = jnp.float32
BF16 = jnp.bfloat16
VMEM_LIMIT = 48 * 1024 * 1024


def dot(a, b):
    return lax.dot_general(a, b, (((1,), (0,)), ((), ())), preferred_element_type=F32)


def dot_nt(a, b):
    return lax.dot_general(a, b, (((1,), (1,)), ((), ())), preferred_element_type=F32)


def dot_tn(a, b):
    return lax.dot_general(a, b, (((0,), (0,)), ((), ())), preferred_element_type=F32)


def doc_of(info, count, pos):
    total = jnp.zeros_like(pos)
    for i in range(count):
        total = total + jnp.where(info[i] <= pos, 1, 0)
    return total


def same(a, b):
    return jnp.where(a == b, F32(1.0), F32(0.0))


def column_docs(info, count, start, size):
    return doc_of(info, count, start + lax.broadcasted_iota(jnp.int32, (size, 1), 0))


def row_docs(info, count, start, size):
    return doc_of(info, count, start + lax.broadcasted_iota(jnp.int32, (1, size), 1))


def causal_masks(info, count, start, transposed):
    cols = [column_docs(info, count, start + i * SUB, SUB) for i in range(BLK // SUB)]
    rows = [row_docs(info, count, start + i * SUB, SUB) for i in range(BLK // SUB)]
    down = lax.broadcasted_iota(jnp.int32, (SUB, SUB), 0)
    over = lax.broadcasted_iota(jnp.int32, (SUB, SUB), 1)
    masks = []
    for r in range(BLK // SUB):
        line = []
        for c in range(BLK // SUB):
            equal = cols[r] == rows[c]
            if r == c:
                line.append(equal & ((down <= over) if transposed else (over <= down)))
            elif (r < c) == transposed:
                line.append(equal)
            else:
                line.append(None)
        masks.append(line)
    return masks


def lane_sums(x):
    return jnp.sum(x.T, axis=0, keepdims=True)


def to_columns(row):
    return jnp.broadcast_to(row, (HEAD_DIM, row.shape[1])).T


def head_slice(h):
    return slice(h * HEAD_DIM, (h + 1) * HEAD_DIM)


def key_state_kernel(count, heads, info, k_ref, v_ref, before_ref, total_ref, state):
    b = pl.program_id(0)

    @pl.when(b == 0)
    def _():
        state[...] = jnp.zeros_like(state)

    start = info[count] + b * BLK
    last_doc = doc_of(info, count, start + BLK - 1)
    keep_out = same(column_docs(info, count, start, BLK), last_doc).astype(BF16)
    carry = same(doc_of(info, count, start - 1), last_doc)
    for h in range(heads):
        before_ref[0, h] = state[h]
        element = dot_tn(k_ref[:, head_slice(h)] * keep_out, v_ref[:, head_slice(h)])
        state[h] = element + carry * state[h]
    total_ref[...] = state[...]


def attention_kernel(
    count, heads, info, q_ref, k_ref, v_ref, before_ref, into_ref, attn_ref, square_ref, low_ref
):
    b = pl.program_id(0)
    first = info[count]
    start = first + b * BLK
    prior = doc_of(info, count, start - 1)
    carry = same(prior, doc_of(info, count, first - 1))
    masks = causal_masks(info, count, start, False)
    keep_in = [
        same(column_docs(info, count, start + r * SUB, SUB), prior) for r in range(BLK // SUB)
    ]
    squares = [jnp.zeros((SUB, HEAD_DIM), F32) for _ in range(BLK // SUB)]
    for h in range(heads):
        low = (before_ref[0, h] + carry * into_ref[h]).astype(BF16)
        low_ref[0, h] = low
        for r in range(BLK // SUB):
            rows = slice(r * SUB, (r + 1) * SUB)
            q = q_ref[rows, head_slice(h)]
            out = keep_in[r] * dot(q, low)
            for c in range(r + 1):
                cols = slice(c * SUB, (c + 1) * SUB)
                scores = dot_nt(q, k_ref[cols, head_slice(h)])
                probs = jnp.where(masks[r][c], scores, 0.0).astype(BF16)
                out = out + dot(probs, v_ref[cols, head_slice(h)])
            attn_ref[rows, head_slice(h)] = out
            squares[r] = squares[r] + out * out
    for r in range(BLK // SUB):
        square_ref[:, r * SUB : (r + 1) * SUB] = lane_sums(squares[r])


def cross_kernel(heads, mix_ref, gate_ref, attn_ref, cross_ref):
    total = jnp.zeros((BLK, HEAD_DIM), F32)
    for h in range(heads):
        at = head_slice(h)
        total = total + mix_ref[:, at].astype(F32) * gate_ref[:, at].astype(F32) * attn_ref[:, at]
    cross_ref[...] = lane_sums(total)


def grad_attn_kernel(
    count,
    heads,
    width,
    info,
    mix_ref,
    gate_ref,
    attn_ref,
    q_ref,
    square_ref,
    cross_ref,
    grad_ref,
    gate_grad_ref,
    after_ref,
    total_ref,
    state,
):
    @pl.when(pl.program_id(0) == 0)
    def _():
        state[...] = jnp.zeros_like(state)

    b = pl.num_programs(0) - 1 - pl.program_id(0)
    start = info[count] + b * BLK
    prior = doc_of(info, count, start - 1)
    keep_in = same(column_docs(info, count, start, BLK), prior).astype(BF16)
    carry = same(doc_of(info, count, start + BLK - 1), prior)
    rms = jnp.sqrt(square_ref[...] / width + EPS)
    inverse = to_columns(1.0 / rms)
    pull = to_columns(cross_ref[...] / (width * (rms * rms * rms)))
    for h in range(heads):
        at = head_slice(h)
        mix = mix_ref[:, at].astype(F32)
        attn = attn_ref[:, at]
        gate_grad_ref[:, at] = (mix * attn * inverse).astype(BF16)
        grad = (mix * gate_ref[:, at].astype(F32) * inverse - attn * pull).astype(BF16)
        grad_ref[:, at] = grad
        after_ref[0, h] = state[h]
        state[h] = dot_tn(q_ref[:, at] * keep_in, grad) + carry * state[h]
    total_ref[...] = state[...]


def grad_query_kernel(count, heads, info, grad_ref, k_ref, v_ref, low_ref, out_ref):
    start = info[count] + pl.program_id(0) * BLK
    prior = doc_of(info, count, start - 1)
    masks = causal_masks(info, count, start, False)
    keep_in = [
        same(column_docs(info, count, start + r * SUB, SUB), prior) for r in range(BLK // SUB)
    ]
    for h in range(heads):
        at = head_slice(h)
        for r in range(BLK // SUB):
            rows = slice(r * SUB, (r + 1) * SUB)
            grad = grad_ref[rows, at]
            out = keep_in[r] * dot_nt(grad, low_ref[0, h])
            for c in range(r + 1):
                cols = slice(c * SUB, (c + 1) * SUB)
                scores = dot_nt(grad, v_ref[cols, at])
                dprob = jnp.where(masks[r][c], scores, 0.0).astype(BF16)
                out = out + dot(dprob, k_ref[cols, at])
            out_ref[rows, at] = out.astype(BF16)


def grad_key_value_kernel(
    count, heads, length, info, grad_ref, q_ref, k_ref, v_ref, after_ref, into_ref, dk_ref, dv_ref
):
    first = info[count]
    start = first + pl.program_id(0) * BLK
    last_doc = doc_of(info, count, start + BLK - 1)
    carry = same(last_doc, doc_of(info, count, first + length - 1))
    masks = causal_masks(info, count, start, True)
    keep_out = [
        same(column_docs(info, count, start + r * SUB, SUB), last_doc) for r in range(BLK // SUB)
    ]
    for h in range(heads):
        at = head_slice(h)
        low = (after_ref[0, h] + carry * into_ref[h]).astype(BF16)
        for r in range(BLK // SUB):
            rows = slice(r * SUB, (r + 1) * SUB)
            k = k_ref[rows, at]
            v = v_ref[rows, at]
            dk = keep_out[r] * dot_nt(v, low)
            dv = keep_out[r] * dot(k, low)
            for c in range(r, BLK // SUB):
                cols = slice(c * SUB, (c + 1) * SUB)
                q = q_ref[cols, at]
                grad = grad_ref[cols, at]
                dprob = jnp.where(masks[r][c], dot_nt(v, grad), 0.0).astype(BF16)
                probs = jnp.where(masks[r][c], dot_nt(k, q), 0.0).astype(BF16)
                dk = dk + dot(dprob, q)
                dv = dv + dot(probs, grad)
            dk_ref[rows, at] = dk.astype(BF16)
            dv_ref[rows, at] = dv.astype(BF16)


def call(kernel, name, info, args, in_specs, outs, out_specs, scratch=(), flops=0):
    nblocks = max(a.shape[0] for a in args if a.ndim == 2) // BLK
    size = sum(a.size * a.dtype.itemsize for a in list(args) + list(outs))
    return pl.pallas_call(
        kernel,
        grid_spec=pltpu.PrefetchScalarGridSpec(
            num_scalar_prefetch=1,
            grid=(nblocks,),
            in_specs=in_specs,
            out_specs=out_specs,
            scratch_shapes=list(scratch),
        ),
        out_shape=outs,
        name=name,
        cost_estimate=pl.CostEstimate(flops=flops, bytes_accessed=size, transcendentals=0),
        compiler_params=pltpu.CompilerParams(vmem_limit_bytes=VMEM_LIMIT),
    )(info, *args)


def shaped(shape, dtype):
    return jax.ShapeDtypeStruct(shape, dtype)


def flip(a, axis, bit):
    return lax.ppermute(a, axis, [(i, i ^ bit) for i in range(lax.axis_size(axis))])


def body(out_grad, out_weight, queries, key_rows, value_rows, gate_out, doc_starts):
    length, width = queries.shape
    heads = width // HEAD_DIM
    nblocks = length // BLK
    count = doc_starts.shape[0]
    nseq = lax.axis_size("seq")
    full_width = width * lax.axis_size("head")
    place = lax.axis_index("seq")
    first = place * length
    info = jnp.concatenate([doc_starts, first[None].astype(jnp.int32)])

    def doc_at(pos):
        return jnp.sum((doc_starts <= pos).astype(jnp.int32))

    block = pl.BlockSpec((BLK, width), lambda b, s: (b, 0))
    line = pl.BlockSpec((1, BLK), lambda b, s: (0, b))
    states = pl.BlockSpec((1, heads, HEAD_DIM, HEAD_DIM), lambda b, s: (b, 0, 0, 0))
    state = pl.BlockSpec((heads, HEAD_DIM, HEAD_DIM), lambda b, s: (0, 0, 0))
    one_state = shaped((heads, HEAD_DIM, HEAD_DIM), F32)
    all_states = shaped((nblocks, heads, HEAD_DIM, HEAD_DIM), F32)
    low_states = shaped((nblocks, heads, HEAD_DIM, HEAD_DIM), BF16)
    tokens16 = shaped((length, width), BF16)
    tokens32 = shaped((length, width), F32)
    row = shaped((1, length), F32)
    scratch = [pltpu.VMEM((heads, HEAD_DIM, HEAD_DIM), F32)]
    unit = 2 * length * width * HEAD_DIM
    intra = 2 * length * width * BLK

    rows_all = lax.all_gather(out_grad, "head", axis=0, tiled=True)

    with jax.named_scope("key_states"):
        before, key_total = call(
            functools.partial(key_state_kernel, count, heads),
            "key_states",
            info,
            [key_rows, value_rows],
            [block, block],
            [all_states, one_state],
            [states, state],
            scratch,
            unit,
        )
    key_totals = lax.all_gather(key_total, "seq")
    into = jnp.zeros((heads, HEAD_DIM, HEAD_DIM), F32)
    for other in range(nseq):
        takes = (other < place) & (doc_at((other + 1) * length - 1) == doc_at(first - 1))
        into = into + jnp.where(takes, key_totals[other], 0.0)
    with jax.named_scope("attention"):
        attn, square, low = call(
            functools.partial(attention_kernel, count, heads),
            "attention",
            info,
            [queries, key_rows, value_rows, before, into],
            [block, block, block, states, state],
            [tokens32, row, low_states],
            [block, line, states],
            (),
            2 * intra,
        )
    square = lax.psum(square, "head")

    mix = lax.dot_general(
        rows_all, out_weight, (((1,), (1,)), ((), ())), preferred_element_type=F32
    ).astype(BF16)

    with jax.named_scope("cross"):
        cross = call(
            lambda info, *refs: cross_kernel(heads, *refs),
            "cross",
            info,
            [mix, gate_out, attn],
            [block, block, block],
            [row],
            [line],
        )[0]
    n_head = lax.axis_size("head")
    bit = 1
    while bit < n_head:
        cross = cross + flip(cross, "head", bit)
        bit *= 2

    back = lambda spec_shape, f: pl.BlockSpec(spec_shape, lambda b, s: f(nblocks - 1 - b))
    block_r = back((BLK, width), lambda b: (b, 0))
    line_r = back((1, BLK), lambda b: (0, b))
    states_r = back((1, heads, HEAD_DIM, HEAD_DIM), lambda b: (b, 0, 0, 0))
    with jax.named_scope("grad_attn"):
        grad, grad_gate, after, query_total = call(
            functools.partial(grad_attn_kernel, count, heads, full_width),
            "grad_attn",
            info,
            [mix, gate_out, attn, queries, square, cross],
            [block_r, block_r, block_r, block_r, line_r, line_r],
            [tokens16, tokens16, all_states, one_state],
            [block_r, block_r, states_r, state],
            scratch,
            unit,
        )
    last = first + length - 1
    out_of = jnp.zeros((heads, HEAD_DIM, HEAD_DIM), F32)
    for step in range(1, nseq):
        other = place ^ step
        takes = (other > place) & (doc_at(other * length - 1) == doc_at(last))
        out_of = out_of + jnp.where(takes, flip(query_total, "seq", step), 0.0)
    with jax.named_scope("grad_queries"):
        grad_queries = call(
            functools.partial(grad_query_kernel, count, heads),
            "grad_queries",
            info,
            [grad, key_rows, value_rows, low],
            [block, block, block, states],
            [tokens16],
            [block],
            (),
            2 * intra,
        )[0]
    with jax.named_scope("grad_keys_values"):
        grad_keys, grad_values = call(
            functools.partial(grad_key_value_kernel, count, heads, length),
            "grad_keys_values",
            info,
            [grad, queries, key_rows, value_rows, after, out_of],
            [block, block, block, block, states, state],
            [tokens16, tokens16],
            [block, block],
            (),
            4 * intra,
        )
    return (grad_queries, grad_keys, grad_values, grad_gate)


def solution(mesh):
    return jax.shard_map(
        body,
        mesh=mesh,
        in_specs=(
            P(("seq", "head"), None),
            P("head", None),
            P("seq", "head"),
            P("seq", "head"),
            P("seq", "head"),
            P("seq", "head"),
            P(),
        ),
        out_specs=(P("seq", "head"), P("seq", "head"), P("seq", "head"), P("seq", "head")),
        check_vma=False,
    )
```

```python
import functools

import jax
import jax.numpy as jnp
from jax import lax
from jax.experimental import pallas as pl
from jax.experimental.pallas import tpu as pltpu
from jax.sharding import PartitionSpec as P

HEAD_DIM = 128
BLK = 512
SUB = 256
EPS = 1e-06
F32 = jnp.float32
BF16 = jnp.bfloat16
VMEM_LIMIT = 56 * 1024 * 1024
PROJECT_VMEM = 32 * 1024 * 1024
SHARE = 4
PIECES = 2


def dot(a, b):
    return lax.dot_general(a, b, (((1,), (0,)), ((), ())), preferred_element_type=F32)


def dot_nt(a, b):
    return lax.dot_general(a, b, (((1,), (1,)), ((), ())), preferred_element_type=F32)


def dot_tn(a, b):
    return lax.dot_general(a, b, (((0,), (0,)), ((), ())), preferred_element_type=F32)


def doc_of(info, count, pos):
    total = jnp.zeros_like(pos)
    for i in range(count):
        total = total + jnp.where(info[i] <= pos, 1, 0)
    return total


def same(a, b):
    return jnp.where(a == b, F32(1.0), F32(0.0))


def column_docs(info, count, start, size):
    return doc_of(info, count, start + lax.broadcasted_iota(jnp.int32, (size, 1), 0))


def row_docs(info, count, start, size):
    return doc_of(info, count, start + lax.broadcasted_iota(jnp.int32, (1, size), 1))


def causal_masks(info, count, start, transposed):
    cols = [column_docs(info, count, start + i * SUB, SUB) for i in range(BLK // SUB)]
    rows = [row_docs(info, count, start + i * SUB, SUB) for i in range(BLK // SUB)]
    down = lax.broadcasted_iota(jnp.int32, (SUB, SUB), 0)
    over = lax.broadcasted_iota(jnp.int32, (SUB, SUB), 1)
    masks = []
    for r in range(BLK // SUB):
        line = []
        for c in range(BLK // SUB):
            equal = cols[r] == rows[c]
            if r == c:
                line.append(equal & ((down <= over) if transposed else (over <= down)))
            elif (r < c) == transposed:
                line.append(equal)
            else:
                line.append(None)
        masks.append(line)
    return masks


def lane_sums(x):
    return jnp.sum(x.T, axis=0, keepdims=True)


def to_columns(row):
    return jnp.broadcast_to(row, (HEAD_DIM, row.shape[1])).T


def head_slice(h):
    return slice(h * HEAD_DIM, (h + 1) * HEAD_DIM)


def key_state_kernel(count, heads, info, k_ref, v_ref, before_ref, total_ref, state):
    b = pl.program_id(0)

    @pl.when(b == 0)
    def _():
        state[...] = jnp.zeros_like(state)

    start = info[count] + b * BLK
    last_doc = doc_of(info, count, start + BLK - 1)
    keep_out = same(column_docs(info, count, start, BLK), last_doc).astype(BF16)
    carry = same(doc_of(info, count, start - 1), last_doc)
    for h in range(heads):
        before_ref[0, h] = state[h]
        element = dot_tn(k_ref[:, head_slice(h)] * keep_out, v_ref[:, head_slice(h)])
        state[h] = element + carry * state[h]
    total_ref[...] = state[...]


def attention_kernel(
    count, heads, info, q_ref, k_ref, v_ref, before_ref, into_ref, attn_ref, square_ref, low_ref
):
    b = pl.program_id(0)
    first = info[count]
    start = first + b * BLK
    prior = doc_of(info, count, start - 1)
    carry = same(prior, doc_of(info, count, first - 1))
    masks = causal_masks(info, count, start, False)
    keep_in = [
        same(column_docs(info, count, start + r * SUB, SUB), prior) for r in range(BLK // SUB)
    ]
    squares = [jnp.zeros((SUB, HEAD_DIM), F32) for _ in range(BLK // SUB)]
    for h in range(heads):
        low = (before_ref[0, h] + carry * into_ref[h]).astype(BF16)
        low_ref[0, h] = low
        for r in range(BLK // SUB):
            rows = slice(r * SUB, (r + 1) * SUB)
            q = q_ref[rows, head_slice(h)]
            out = keep_in[r] * dot(q, low)
            for c in range(r + 1):
                cols = slice(c * SUB, (c + 1) * SUB)
                scores = dot_nt(q, k_ref[cols, head_slice(h)])
                probs = jnp.where(masks[r][c], scores, 0.0).astype(BF16)
                out = out + dot(probs, v_ref[cols, head_slice(h)])
            attn_ref[rows, head_slice(h)] = out
            squares[r] = squares[r] + out * out
    for r in range(BLK // SUB):
        square_ref[:, r * SUB : (r + 1) * SUB] = lane_sums(squares[r])


def cross_kernel(heads, mix_ref, gate_ref, attn_ref, cross_ref):
    total = jnp.zeros((BLK, HEAD_DIM), F32)
    for h in range(heads):
        at = head_slice(h)
        total = total + mix_ref[:, at].astype(F32) * gate_ref[:, at].astype(F32) * attn_ref[:, at]
    cross_ref[...] = lane_sums(total)


def grad_attn_kernel(
    count,
    heads,
    width,
    info,
    mix_ref,
    gate_ref,
    attn_ref,
    q_ref,
    sums_ref,
    grad_ref,
    gate_grad_ref,
    after_ref,
    total_ref,
    state,
):
    @pl.when(pl.program_id(0) == 0)
    def _():
        state[...] = jnp.zeros_like(state)

    b = pl.num_programs(0) - 1 - pl.program_id(0)
    start = info[count] + b * BLK
    prior = doc_of(info, count, start - 1)
    keep_in = same(column_docs(info, count, start, BLK), prior).astype(BF16)
    carry = same(doc_of(info, count, start + BLK - 1), prior)
    rms = jnp.sqrt(sums_ref[0:1, :] / width + EPS)
    inverse = to_columns(1.0 / rms)
    pull = to_columns(sums_ref[1:2, :] / (width * (rms * rms * rms)))
    for h in range(heads):
        at = head_slice(h)
        mix = mix_ref[:, at].astype(F32)
        attn = attn_ref[:, at]
        gate_grad_ref[:, at] = (mix * attn * inverse).astype(BF16)
        grad = (mix * gate_ref[:, at].astype(F32) * inverse - attn * pull).astype(BF16)
        grad_ref[:, at] = grad
        after_ref[0, h] = state[h]
        state[h] = dot_tn(q_ref[:, at] * keep_in, grad) + carry * state[h]
    total_ref[...] = state[...]


def grad_query_kernel(count, heads, info, grad_ref, k_ref, v_ref, low_ref, out_ref):
    start = info[count] + pl.program_id(0) * BLK
    prior = doc_of(info, count, start - 1)
    masks = causal_masks(info, count, start, False)
    keep_in = [
        same(column_docs(info, count, start + r * SUB, SUB), prior) for r in range(BLK // SUB)
    ]
    for h in range(heads):
        at = head_slice(h)
        for r in range(BLK // SUB):
            rows = slice(r * SUB, (r + 1) * SUB)
            grad = grad_ref[rows, at]
            out = keep_in[r] * dot_nt(grad, low_ref[0, h])
            for c in range(r + 1):
                cols = slice(c * SUB, (c + 1) * SUB)
                scores = dot_nt(grad, v_ref[cols, at])
                dprob = jnp.where(masks[r][c], scores, 0.0).astype(BF16)
                out = out + dot(dprob, k_ref[cols, at])
            out_ref[rows, at] = out.astype(BF16)


def grad_key_value_kernel(
    count, heads, length, info, grad_ref, q_ref, k_ref, v_ref, after_ref, into_ref, dk_ref, dv_ref
):
    first = info[count]
    start = first + pl.program_id(0) * BLK
    last_doc = doc_of(info, count, start + BLK - 1)
    carry = same(last_doc, doc_of(info, count, first + length - 1))
    masks = causal_masks(info, count, start, True)
    keep_out = [
        same(column_docs(info, count, start + r * SUB, SUB), last_doc) for r in range(BLK // SUB)
    ]
    for h in range(heads):
        at = head_slice(h)
        low = (after_ref[0, h] + carry * into_ref[h]).astype(BF16)
        for r in range(BLK // SUB):
            rows = slice(r * SUB, (r + 1) * SUB)
            k = k_ref[rows, at]
            v = v_ref[rows, at]
            dk = keep_out[r] * dot_nt(v, low)
            dv = keep_out[r] * dot(k, low)
            for c in range(r, BLK // SUB):
                cols = slice(c * SUB, (c + 1) * SUB)
                q = q_ref[cols, at]
                grad = grad_ref[cols, at]
                dprob = jnp.where(masks[r][c], dot_nt(v, grad), 0.0).astype(BF16)
                probs = jnp.where(masks[r][c], dot_nt(k, q), 0.0).astype(BF16)
                dk = dk + dot(dprob, q)
                dv = dv + dot(probs, grad)
            dk_ref[rows, at] = dk.astype(BF16)
            dv_ref[rows, at] = dv.astype(BF16)


def project_kernel(depth, info, own_ref, pair_ref, *refs):
    *parts, out_ref = refs
    rows = own_ref.shape[0]
    side = info[0]
    for place, ref in ((side, own_ref), (1 - side, pair_ref)):
        total = None
        for j, part in enumerate(parts):
            if len(parts) == 1:
                left = ref[...]
            else:
                left = ref[:, pl.ds(pl.multiple_of((info[1] ^ j) * depth, depth), depth)]
            term = dot_nt(left, part[...])
            total = term if total is None else total + term
        out_ref[pl.ds(pl.multiple_of(place * rows, rows), rows), :] = total.astype(BF16)


def project(info, own, pair, parts):
    features, depth = parts[0].shape
    rows = own.shape[0]
    args = [own, pair, *parts]
    size = sum(a.size * 2 for a in args) + 4 * rows * features
    return pl.pallas_call(
        functools.partial(project_kernel, depth),
        grid_spec=pltpu.PrefetchScalarGridSpec(
            num_scalar_prefetch=1,
            grid=(1,),
            in_specs=[pl.BlockSpec(a.shape, lambda i, s: (0, 0)) for a in args],
            out_specs=pl.BlockSpec((2 * rows, features), lambda i, s: (0, 0)),
        ),
        out_shape=jax.ShapeDtypeStruct((2 * rows, features), BF16),
        name="project",
        cost_estimate=pl.CostEstimate(
            flops=4 * rows * features * own.shape[1], bytes_accessed=size, transcendentals=0
        ),
        compiler_params=pltpu.CompilerParams(vmem_limit_bytes=PROJECT_VMEM),
    )(info, *args)


def after(arrays, *done):
    return lax.optimization_barrier((tuple(arrays), done))[0]


def grad_mixture(out_grad, out_weight, length, early, late):
    n_head = lax.axis_size("head")
    n_pairs = n_head // 2
    rows, depth = out_grad.shape
    width = out_weight.shape[0]
    half = width // PIECES
    part_depth = depth // SHARE
    me = lax.axis_index("head")
    side, pair = me % 2, me // 2
    slot = lax.axis_index("seq") % SHARE
    info = jnp.stack([side, slot]).astype(jnp.int32)
    hops = sorted(range(1, n_pairs), key=lambda k: (bin(k).count("1"), -k))
    order = [(0, hop) for hop in hops if hop & (hop - 1) == 0]
    order += [(1, hop) for hop in hops[:1]]
    order += [(0, hop) for hop in hops if hop & (hop - 1) != 0]
    order += [(1, hop) for hop in hops[1:]]
    waves = [order[i : i + 2] for i in range(0, len(order), 2)]

    fetched = {
        (piece, 0): lax.dynamic_slice(
            out_weight, (piece * half, slot * part_depth), (half, part_depth)
        )
        for piece in range(PIECES)
    }
    products = []
    shards = {}
    own_rows = out_grad
    pair_rows = None
    beside = None
    ready = ()
    exchanged = []
    for step in range(len(waves) + 2):
        wave = waves[step] if step < len(waves) else []
        sources = [fetched[(piece, hop ^ (hop & -hop))] for piece, hop in wave]
        sources = after(sources, *ready) if ready else sources
        landing = [
            flip(source, "head", 2 * (hop & -hop)) for source, (piece, hop) in zip(sources, wave)
        ]
        if step == 0:
            pair_rows = flip(out_grad, "head", 1)
        previous = waves[step - 1] if 0 < step <= len(waves) else []
        mine = [fetched[key] for key in previous]
        mine = after(mine, *ready) if ready and mine else mine
        across = [flip(part, "seq", 2) for part in mine]
        beside_mine = [flip(part, "seq", 1) for part in mine]
        if exchanged:
            keys, mine_e, across_e, beside_e = exchanged
            last = [flip(part, "seq", 1) for part in across_e]
            for key, m, x, c, l in zip(keys, mine_e, across_e, beside_e, last):
                shards[key] = [m, c, x, l]
                product = project(info, own_rows, pair_rows, shards[key])
                products.append((key, flip(product, "head", 2 * key[1])))
        if step == 0:
            extra = early()
        elif step == 1:
            extra = late()
        elif step == 2:
            extra = project(info, own_rows, pair_rows, [out_weight])
            own_product = extra
        else:
            extra = ()
        exchanged = (previous, mine, across, beside_mine) if previous else ()
        for key, part in zip(wave, landing):
            fetched[key] = part
        ready = tuple(landing) + tuple(across) + tuple(jax.tree.leaves(extra))
    mix = jnp.zeros((length, width), BF16)
    mix = lax.dynamic_update_slice(mix, own_product, (pair * 2 * rows, 0))
    for (piece, hop), product in products:
        mix = lax.dynamic_update_slice(mix, product, ((pair ^ hop) * 2 * rows, piece * half))
    return mix


def call(kernel, name, info, args, in_specs, outs, out_specs, scratch=(), flops=0):
    nblocks = max(a.shape[0] for a in args if a.ndim == 2) // BLK
    size = sum(a.size * a.dtype.itemsize for a in list(args) + list(outs))
    return pl.pallas_call(
        kernel,
        grid_spec=pltpu.PrefetchScalarGridSpec(
            num_scalar_prefetch=1,
            grid=(nblocks,),
            in_specs=in_specs,
            out_specs=out_specs,
            scratch_shapes=list(scratch),
        ),
        out_shape=outs,
        name=name,
        cost_estimate=pl.CostEstimate(flops=flops, bytes_accessed=size, transcendentals=0),
        compiler_params=pltpu.CompilerParams(vmem_limit_bytes=VMEM_LIMIT),
    )(info, *args)


def shaped(shape, dtype):
    return jax.ShapeDtypeStruct(shape, dtype)


def flip(a, axis, bit):
    return lax.ppermute(a, axis, [(i, i ^ bit) for i in range(lax.axis_size(axis))])


def body(out_grad, out_weight, queries, key_rows, value_rows, gate_out, doc_starts):
    length, width = queries.shape
    heads = width // HEAD_DIM
    nblocks = length // BLK
    count = doc_starts.shape[0]
    nseq = lax.axis_size("seq")
    full_width = width * lax.axis_size("head")
    place = lax.axis_index("seq")
    first = place * length
    info = jnp.concatenate([doc_starts, first[None].astype(jnp.int32)])

    def doc_at(pos):
        return jnp.sum((doc_starts <= pos).astype(jnp.int32))

    block = pl.BlockSpec((BLK, width), lambda b, s: (b, 0))
    line = pl.BlockSpec((1, BLK), lambda b, s: (0, b))
    states = pl.BlockSpec((1, heads, HEAD_DIM, HEAD_DIM), lambda b, s: (b, 0, 0, 0))
    state = pl.BlockSpec((heads, HEAD_DIM, HEAD_DIM), lambda b, s: (0, 0, 0))
    one_state = shaped((heads, HEAD_DIM, HEAD_DIM), F32)
    all_states = shaped((nblocks, heads, HEAD_DIM, HEAD_DIM), F32)
    low_states = shaped((nblocks, heads, HEAD_DIM, HEAD_DIM), BF16)
    tokens16 = shaped((length, width), BF16)
    tokens32 = shaped((length, width), F32)
    row = shaped((1, length), F32)
    scratch = [pltpu.VMEM((heads, HEAD_DIM, HEAD_DIM), F32)]
    unit = 2 * length * width * HEAD_DIM
    intra = 2 * length * width * BLK

    kept = {}

    def early():
        with jax.named_scope("key_states"):
            before, key_total = call(
                functools.partial(key_state_kernel, count, heads),
                "key_states",
                info,
                [key_rows, value_rows],
                [block, block],
                [all_states, one_state],
                [states, state],
                scratch,
                unit,
            )
        key_totals = lax.all_gather(key_total, "seq")
        into = jnp.zeros((heads, HEAD_DIM, HEAD_DIM), F32)
        for other in range(nseq):
            takes = (other < place) & (doc_at((other + 1) * length - 1) == doc_at(first - 1))
            into = into + jnp.where(takes, key_totals[other], 0.0)
        kept["before"], kept["into"] = before, into
        return before

    def late():
        with jax.named_scope("attention"):
            kept["attn"], kept["square"], kept["low"] = call(
                functools.partial(attention_kernel, count, heads),
                "attention",
                info,
                [queries, key_rows, value_rows, kept["before"], kept["into"]],
                [block, block, block, states, state],
                [tokens32, row, low_states],
                [block, line, states],
                (),
                2 * intra,
            )
        return kept["square"]

    mix = grad_mixture(out_grad, out_weight, length, early, late)
    attn, square, low = kept["attn"], kept["square"], kept["low"]

    with jax.named_scope("cross"):
        cross = call(
            lambda info, *refs: cross_kernel(heads, *refs),
            "cross",
            info,
            [mix, gate_out, attn],
            [block, block, block],
            [row],
            [line],
        )[0]
    n_head = lax.axis_size("head")
    sums = jnp.concatenate([square, cross], axis=0)
    bit = 1
    while bit < n_head:
        sums = sums + flip(sums, "head", bit)
        bit *= 2

    back = lambda spec_shape, f: pl.BlockSpec(spec_shape, lambda b, s: f(nblocks - 1 - b))
    block_r = back((BLK, width), lambda b: (b, 0))
    line_r = back((2, BLK), lambda b: (0, b))
    states_r = back((1, heads, HEAD_DIM, HEAD_DIM), lambda b: (b, 0, 0, 0))
    with jax.named_scope("grad_attn"):
        grad, grad_gate, after, query_total = call(
            functools.partial(grad_attn_kernel, count, heads, full_width),
            "grad_attn",
            info,
            [mix, gate_out, attn, queries, sums],
            [block_r, block_r, block_r, block_r, line_r],
            [tokens16, tokens16, all_states, one_state],
            [block_r, block_r, states_r, state],
            scratch,
            unit,
        )
    last = first + length - 1
    out_of = jnp.zeros((heads, HEAD_DIM, HEAD_DIM), F32)
    for step in range(1, nseq):
        other = place ^ step
        takes = (other > place) & (doc_at(other * length - 1) == doc_at(last))
        out_of = out_of + jnp.where(takes, flip(query_total, "seq", step), 0.0)
    with jax.named_scope("grad_queries"):
        grad_queries = call(
            functools.partial(grad_query_kernel, count, heads),
            "grad_queries",
            info,
            [grad, key_rows, value_rows, low],
            [block, block, block, states],
            [tokens16],
            [block],
            (),
            2 * intra,
        )[0]
    with jax.named_scope("grad_keys_values"):
        grad_keys, grad_values = call(
            functools.partial(grad_key_value_kernel, count, heads, length),
            "grad_keys_values",
            info,
            [grad, queries, key_rows, value_rows, after, out_of],
            [block, block, block, block, states, state],
            [tokens16, tokens16],
            [block, block],
            (),
            4 * intra,
        )
    return (grad_queries, grad_keys, grad_values, grad_gate)


def solution(mesh):
    return jax.shard_map(
        body,
        mesh=mesh,
        in_specs=(
            P(("seq", "head"), None),
            P("head", None),
            P("seq", "head"),
            P("seq", "head"),
            P("seq", "head"),
            P("seq", "head"),
            P(),
        ),
        out_specs=(P("seq", "head"), P("seq", "head"), P("seq", "head"), P("seq", "head")),
        check_vma=False,
    )
```

```python
import functools

import jax
import jax.numpy as jnp
from jax import lax
from jax.experimental import pallas as pl
from jax.experimental.pallas import tpu as pltpu
from jax.sharding import PartitionSpec as P

HEAD_DIM = 128
BLK = 512
CHUNK = 256
EPS = 1e-06
F32 = jnp.float32
BF16 = jnp.bfloat16
VMEM_LIMIT = 16 * 1024 * 1024
PROJECT_VMEM = 24 * 1024 * 1024
PIECES = 2
COST_SCALE = 1.15e9


def dot(a, b):
    return lax.dot_general(a, b, (((1,), (0,)), ((), ())), preferred_element_type=F32)


def dot_nt(a, b):
    return lax.dot_general(a, b, (((1,), (1,)), ((), ())), preferred_element_type=F32)


def dot_tn(a, b):
    return lax.dot_general(a, b, (((0,), (0,)), ((), ())), preferred_element_type=F32)


def doc_of(info, count, pos):
    total = jnp.zeros_like(pos)
    for i in range(count):
        total = total + jnp.where(info[i] <= pos, 1, 0)
    return total


def same(a, b):
    return jnp.where(a == b, F32(1.0), F32(0.0))


def column_docs(info, count, start, size):
    return doc_of(info, count, start + lax.broadcasted_iota(jnp.int32, (size, 1), 0))


def row_docs(info, count, start, size):
    return doc_of(info, count, start + lax.broadcasted_iota(jnp.int32, (1, size), 1))


def causal_mask(info, count, start, transposed):
    down = lax.broadcasted_iota(jnp.int32, (CHUNK, CHUNK), 0)
    over = lax.broadcasted_iota(jnp.int32, (CHUNK, CHUNK), 1)
    equal = column_docs(info, count, start, CHUNK) == row_docs(info, count, start, CHUNK)
    return equal & ((down <= over) if transposed else (over <= down))


def chunk_rows(r):
    return slice(r * CHUNK, (r + 1) * CHUNK)


def lane_sums(x):
    return jnp.sum(x.T, axis=0, keepdims=True)


def to_columns(row):
    return jnp.broadcast_to(row, (HEAD_DIM, row.shape[1])).T


def head_slice(h):
    return slice(h * HEAD_DIM, (h + 1) * HEAD_DIM)


def key_state_kernel(count, heads, info, k_ref, v_ref, before_ref, total_ref, state):
    b = pl.program_id(0)

    @pl.when(b == 0)
    def _():
        state[...] = jnp.zeros_like(state)

    for r in range(BLK // CHUNK):
        rows = chunk_rows(r)
        start = info[count] + b * BLK + r * CHUNK
        last_doc = doc_of(info, count, start + CHUNK - 1)
        keep_out = same(column_docs(info, count, start, CHUNK), last_doc).astype(BF16)
        carry = same(doc_of(info, count, start - 1), last_doc)
        for h in range(heads):
            at = head_slice(h)
            before_ref[r, h] = state[h]
            state[h] = dot_tn(k_ref[rows, at] * keep_out, v_ref[rows, at]) + carry * state[h]
    total_ref[...] = state[...]


def attention_kernel(
    count, heads, info, q_ref, k_ref, v_ref, before_ref, into_ref, attn_ref, square_ref, low_ref
):
    first = info[count]
    for r in range(BLK // CHUNK):
        rows = chunk_rows(r)
        start = first + pl.program_id(0) * BLK + r * CHUNK
        prior = doc_of(info, count, start - 1)
        carry = same(prior, doc_of(info, count, first - 1))
        mask = causal_mask(info, count, start, False)
        keep_in = same(column_docs(info, count, start, CHUNK), prior)
        squares = jnp.zeros((CHUNK, HEAD_DIM), F32)
        for h in range(heads):
            at = head_slice(h)
            low = (before_ref[r, h] + carry * into_ref[h]).astype(BF16)
            low_ref[r, h] = low
            q = q_ref[rows, at]
            probs = jnp.where(mask, dot_nt(q, k_ref[rows, at]), 0.0).astype(BF16)
            out = keep_in * dot(q, low) + dot(probs, v_ref[rows, at])
            attn_ref[rows, at] = out
            squares = squares + out * out
        square_ref[:, rows] = lane_sums(squares)


def mix_heads(heads, info, near_ref, far_ref):
    core = info[info.shape[0] - 1]
    half = heads // 2
    for index, ref in enumerate((near_ref, far_ref)):
        for i in range(half):
            h = (core ^ index) * half + i
            at = pl.ds(pl.multiple_of(h * HEAD_DIM, HEAD_DIM), HEAD_DIM)
            yield ref.at[:, head_slice(i)], at


def cross_kernel(heads, info, near_ref, far_ref, gate_ref, attn_ref, cross_ref):
    total = jnp.zeros((BLK, HEAD_DIM), F32)
    for mix, at in mix_heads(heads, info, near_ref, far_ref):
        total = total + mix[...].astype(F32) * gate_ref[:, at].astype(F32) * attn_ref[:, at]
    cross_ref[...] = lane_sums(total)


def grad_attn_kernel(
    count,
    heads,
    width,
    info,
    near_ref,
    far_ref,
    gate_ref,
    attn_ref,
    q_ref,
    sums_ref,
    grad_ref,
    gate_grad_ref,
    after_ref,
    total_ref,
    state,
):
    @pl.when(pl.program_id(0) == 0)
    def _():
        state[...] = jnp.zeros_like(state)

    b = pl.num_programs(0) - 1 - pl.program_id(0)
    rms = jnp.sqrt(sums_ref[0:1, :] / width + EPS)
    inverse = to_columns(1.0 / rms)
    pull = to_columns(sums_ref[1:2, :] / (width * (rms * rms * rms)))
    for r in reversed(range(BLK // CHUNK)):
        rows = chunk_rows(r)
        start = info[count] + b * BLK + r * CHUNK
        prior = doc_of(info, count, start - 1)
        keep_in = same(column_docs(info, count, start, CHUNK), prior).astype(BF16)
        carry = same(doc_of(info, count, start + CHUNK - 1), prior)
        half = heads // 2
        for i, (mix, at) in enumerate(mix_heads(heads, info, near_ref, far_ref)):
            h = (info[count + 1] ^ (i // half)) * half + i % half
            scaled = mix[rows].astype(F32) * inverse[rows]
            attn = attn_ref[rows, at]
            gate_grad_ref[rows, at] = (scaled * attn).astype(BF16)
            grad = (scaled * gate_ref[rows, at].astype(F32) - attn * pull[rows]).astype(BF16)
            grad_ref[rows, at] = grad
            after_ref[r, h] = state[h]
            state[h] = dot_tn(q_ref[rows, at] * keep_in, grad) + carry * state[h]
    total_ref[...] = state[...]


def grad_query_kernel(count, heads, info, grad_ref, k_ref, v_ref, low_ref, out_ref):
    for r in range(BLK // CHUNK):
        rows = chunk_rows(r)
        start = info[count] + pl.program_id(0) * BLK + r * CHUNK
        prior = doc_of(info, count, start - 1)
        mask = causal_mask(info, count, start, False)
        keep_in = same(column_docs(info, count, start, CHUNK), prior)
        for h in range(heads):
            at = head_slice(h)
            grad = grad_ref[rows, at]
            dprob = jnp.where(mask, dot_nt(grad, v_ref[rows, at]), 0.0).astype(BF16)
            out = keep_in * dot_nt(grad, low_ref[r, h]) + dot(dprob, k_ref[rows, at])
            out_ref[rows, at] = out.astype(BF16)


def grad_key_value_kernel(
    count, heads, length, info, grad_ref, q_ref, k_ref, v_ref, after_ref, into_ref, dk_ref, dv_ref
):
    first = info[count]
    for r in range(BLK // CHUNK):
        rows = chunk_rows(r)
        start = first + pl.program_id(0) * BLK + r * CHUNK
        last_doc = doc_of(info, count, start + CHUNK - 1)
        carry = same(last_doc, doc_of(info, count, first + length - 1))
        mask = causal_mask(info, count, start, True)
        keep_out = same(column_docs(info, count, start, CHUNK), last_doc)
        for h in range(heads):
            at = head_slice(h)
            low = (after_ref[r, h] + carry * into_ref[h]).astype(BF16)
            k, v, q, grad = k_ref[rows, at], v_ref[rows, at], q_ref[rows, at], grad_ref[rows, at]
            dprob = jnp.where(mask, dot_nt(v, grad), 0.0).astype(BF16)
            probs = jnp.where(mask, dot_nt(k, q), 0.0).astype(BF16)
            dk_ref[rows, at] = (keep_out * dot_nt(v, low) + dot(dprob, q)).astype(BF16)
            dv_ref[rows, at] = (keep_out * dot(k, low) + dot(probs, grad)).astype(BF16)


def neighbour_states(total, doc_starts, length, reverse):
    def doc_at(pos):
        return jnp.sum((doc_starts <= pos).astype(jnp.int32))

    place = lax.axis_index("seq")
    mine = doc_at((place + 1) * length - 1 if reverse else place * length - 1)
    into = jnp.zeros_like(total)
    if reverse and lax.axis_size("seq") <= 4:
        for step in range(1, lax.axis_size("seq")):
            source = place ^ step
            edge = doc_at(source * length - 1 + (0 if reverse else length))
            outer = (source > place) if reverse else (source < place)
            sent = total if step == 1 else total.astype(BF16)
            into = into + jnp.where(outer & (edge == mine), flip(sent, "seq", step), 0.0)
        return into
    size = 1
    while size < lax.axis_size("seq"):
        other = flip(total if size == 1 else total.astype(BF16), "seq", size).astype(F32)
        group = place // size
        other_edge = doc_at((group ^ 1) * size * length - 1 + (0 if reverse else size * length))
        my_edge = doc_at(group * size * length - 1 + (0 if reverse else size * length))
        outer = (group % 2 == 0) if reverse else (group % 2 == 1)
        into = into + jnp.where(outer & (other_edge == mine), other, 0.0)
        joined = other_edge == my_edge
        total = jnp.where(
            outer,
            total + jnp.where(joined, other, 0.0),
            other + jnp.where(joined, total, 0.0),
        )
        size *= 2
    return into


def project_kernel(split, info, *refs):
    sets = refs[:4]
    shards = refs[4 : len(refs) - (len(refs) - 4) // (split + 1)]
    outs = refs[4 + len(shards) :]
    rows, depth = sets[0].shape
    part = depth // split
    slot = info[1]
    weights = [
        jnp.concatenate([shards[i * split + j][...] for i in range(len(outs))], axis=0)
        for j in range(split)
    ]
    for index, ref in enumerate(sets):
        total = None
        for j in range(split):
            if split == 1:
                left = ref[...]
            else:
                left = ref[:, pl.ds(pl.multiple_of((slot ^ j) * part, part), part)]
            term = dot_nt(left, weights[j])
            total = term if total is None else total + term
        place = 2 * (info[2] ^ (index // 2)) + (info[0] ^ (index % 2))
        at = pl.ds(pl.multiple_of(place * rows, rows), rows)
        width = total.shape[1] // len(outs)
        for i, out in enumerate(outs):
            out[at, :] = total[:, i * width : (i + 1) * width].astype(BF16)


def project(info, sets, shards):
    split = len(shards[0])
    features = shards[0][0].shape[0]
    rows, depth = sets[0].shape
    args = [*sets, *(part for parts in shards for part in parts)]
    outs = [jax.ShapeDtypeStruct((4 * rows, features), BF16)] * len(shards)
    return pl.pallas_call(
        functools.partial(project_kernel, split),
        grid_spec=pltpu.PrefetchScalarGridSpec(
            num_scalar_prefetch=1,
            grid=(1,),
            in_specs=[pl.BlockSpec(memory_space=pltpu.VMEM) for a in args],
            out_specs=[pl.BlockSpec(memory_space=pltpu.VMEM) for o in outs],
        ),
        out_shape=outs,
        name="project",
        cost_estimate=cost(5.0),
        compiler_params=pltpu.CompilerParams(vmem_limit_bytes=PROJECT_VMEM),
    )(info, *args)


def cost(micros):
    return pl.CostEstimate(
        flops=int(micros * COST_SCALE), bytes_accessed=0, transcendentals=0
    )


def grad_mixture(out_grad, out_weight, length, early, late):
    n_head = lax.axis_size("head")
    n_pairs = n_head // 2
    rows, depth = out_grad.shape
    width = out_weight.shape[0]
    half = width // 2
    piece_size = half // PIECES
    part_depth = depth // 2
    me = lax.axis_index("head")
    side, pair = me % 2, me // 2
    core = lax.axis_index("seq") % 2
    slot = (lax.axis_index("seq") // 2) % 2
    info = jnp.stack([side, slot, core]).astype(jnp.int32)
    hops = sorted(range(1, n_pairs), key=lambda k: (bin(k).count("1"), -k))
    order = [(0, hop) for hop in hops if hop & (hop - 1) == 0]
    order += [(1, hop) for hop in hops[:1]]
    order += [(0, hop) for hop in hops if hop & (hop - 1) != 0]
    order += [(1, hop) for hop in hops[1:]]
    waves = [order[i : i + 2] for i in range(0, len(order), 2)]

    fetched = {
        (piece, 0): lax.dynamic_slice(
            out_weight,
            (core * half + piece * piece_size, slot * part_depth),
            (piece_size, part_depth),
        )
        for piece in range(PIECES)
    }
    sets = [out_grad, flip(out_grad, "head", 1), None, None]
    across = {}
    arrived = {}
    for step in range(len(waves) + 2):
        wave = waves[step] if step < len(waves) else []
        landed = waves[step - 1] if 0 < step <= len(waves) else []
        spread = waves[step - 2] if 1 < step else []
        for piece, hop in wave:
            low = hop & -hop
            fetched[piece, hop] = flip(fetched[piece, hop ^ low], "head", 2 * low)
        for key in landed:
            across[key] = flip(fetched[key], "seq", 2)
        made = []
        if step == 1:
            sets[2] = flip(out_grad, "seq", 1)
            made += [sets[1], early()]
        if step == 2:
            sets[3] = flip(sets[1], "seq", 1)
        if spread:
            shards = [[fetched[key], across[key]] for key in spread]
            products = project(info, sets, shards)
            made += products
            for key, product in zip(spread, products):
                arrived[key] = flip(product, "head", 2 * key[1])
        if step == 2:
            made.append(late(products[0]))
        if step == 3:
            mine = lax.dynamic_slice(out_weight, (core * half, 0), (half, depth))
            arrived[0, 0] = project(info, sets, [[mine]])[0]
            made.append(arrived[0, 0])
        if step < len(waves) + 1:
            names = [key for key in fetched if key not in wave]
            keep, new, far, made = lax.optimization_barrier(
                (
                    [fetched[key] for key in names],
                    [fetched[key] for key in wave],
                    [across[key] for key in landed],
                    made,
                )
            )
            if step == 1:
                sets[1] = made[0]
            fetched.update(zip(names, keep))
            fetched.update(zip(wave, new))
            across.update(zip(landed, far))
    mixes = []
    for source in (None, 1):
        mix = jnp.zeros((length, half), BF16)
        for (piece, hop), product in arrived.items():
            which = core if source is None else 1 - core
            product = lax.dynamic_slice(
                product, (which * 2 * rows, 0), (2 * rows, product.shape[1])
            )
            mix = lax.dynamic_update_slice(
                mix, product, ((pair ^ hop) * 2 * rows, piece * piece_size)
            )
        mixes.append(mix)
    return mixes[0], flip(mixes[1], "seq", 1)


def call(kernel, name, info, args, in_specs, outs, out_specs, scratch=(), micros=3.0):
    nblocks = max(a.shape[0] for a in args if a.ndim == 2) // BLK
    return pl.pallas_call(
        kernel,
        grid_spec=pltpu.PrefetchScalarGridSpec(
            num_scalar_prefetch=1,
            grid=(nblocks,),
            in_specs=in_specs,
            out_specs=out_specs,
            scratch_shapes=list(scratch),
        ),
        out_shape=outs,
        name=name,
        cost_estimate=cost(micros),
        compiler_params=pltpu.CompilerParams(vmem_limit_bytes=VMEM_LIMIT),
    )(info, *args)


def shaped(shape, dtype):
    return jax.ShapeDtypeStruct(shape, dtype)


def flip(a, axis, bit):
    return lax.ppermute(a, axis, [(i, i ^ bit) for i in range(lax.axis_size(axis))])


def subsets(items):
    found = [[]]
    for item in items:
        found += [[*one, item] for one in found]
    return found[1:]


def head_sum(sums):
    bits = [1 << i for i in range(lax.axis_size("head").bit_length() - 1)]
    for group in (bits[1:3], bits[:1], bits[3:]):
        spans = [sum(chosen) for chosen in subsets(group)]
        sums = sums + sum(flip(sums, "head", span) for span in spans) if spans else sums
    return sums


def body(out_grad, out_weight, queries, key_rows, value_rows, gate_out, doc_starts):
    length, width = queries.shape
    heads = width // HEAD_DIM
    nblocks = length // BLK
    count = doc_starts.shape[0]
    full_width = width * lax.axis_size("head")
    place = lax.axis_index("seq")
    first = place * length
    info = jnp.concatenate([doc_starts, jnp.stack([first, place % 2]).astype(jnp.int32)])

    block = pl.BlockSpec((BLK, width), lambda b, s: (b, 0))
    half_block = pl.BlockSpec((BLK, width // 2), lambda b, s: (b, 0))
    line = pl.BlockSpec((1, BLK), lambda b, s: (0, b))
    states = pl.BlockSpec((BLK // CHUNK, heads, HEAD_DIM, HEAD_DIM), lambda b, s: (b, 0, 0, 0))
    state = pl.BlockSpec((heads, HEAD_DIM, HEAD_DIM), lambda b, s: (0, 0, 0))
    one_state = shaped((heads, HEAD_DIM, HEAD_DIM), F32)
    all_states = shaped((length // CHUNK, heads, HEAD_DIM, HEAD_DIM), F32)
    low_states = shaped((length // CHUNK, heads, HEAD_DIM, HEAD_DIM), BF16)
    tokens16 = shaped((length, width), BF16)
    tokens32 = shaped((length, width), F32)
    row = shaped((1, length), F32)
    scratch = [pltpu.VMEM((heads, HEAD_DIM, HEAD_DIM), F32)]

    kept = {}

    def early():
        with jax.named_scope("key_states"):
            before, key_total = call(
                functools.partial(key_state_kernel, count, heads),
                "key_states",
                info,
                [key_rows, value_rows],
                [block, block],
                [all_states, one_state],
                [states, state],
                scratch,
            )
        kept["before"] = before
        kept["into"] = neighbour_states(key_total, doc_starts, length, False)
        return kept["into"]

    def late(product):
        tokens, _ = lax.optimization_barrier((queries, product))
        with jax.named_scope("attention"):
            kept["attn"], kept["square"], kept["low"] = call(
                functools.partial(attention_kernel, count, heads),
                "attention",
                info,
                [tokens, key_rows, value_rows, kept["before"], kept["into"]],
                [block, block, block, states, state],
                [tokens32, row, low_states],
                [block, line, states],
            )
        return kept["square"]

    near, far = grad_mixture(out_grad, out_weight, length, early, late)
    attn, square, low = kept["attn"], kept["square"], kept["low"]

    with jax.named_scope("cross"):
        cross = call(
            functools.partial(cross_kernel, heads),
            "cross",
            info,
            [near, far, gate_out, attn],
            [half_block, half_block, block, block],
            [row],
            [line],
        )[0]

    sums = head_sum(jnp.concatenate([square, cross], axis=0))

    back = lambda spec_shape, f: pl.BlockSpec(spec_shape, lambda b, s: f(nblocks - 1 - b))
    block_r = back((BLK, width), lambda b: (b, 0))
    half_r = back((BLK, width // 2), lambda b: (b, 0))
    line_r = back((2, BLK), lambda b: (0, b))
    states_r = back((BLK // CHUNK, heads, HEAD_DIM, HEAD_DIM), lambda b: (b, 0, 0, 0))
    with jax.named_scope("grad_attn"):
        grad, grad_gate, after, query_total = call(
            functools.partial(grad_attn_kernel, count, heads, full_width),
            "grad_attn",
            info,
            [near, far, gate_out, attn, queries, sums],
            [half_r, half_r, block_r, block_r, block_r, line_r],
            [tokens16, tokens16, all_states, one_state],
            [block_r, block_r, states_r, state],
            scratch,
        )
    out_of = neighbour_states(query_total, doc_starts, length, True)
    with jax.named_scope("grad_queries"):
        grad_queries = call(
            functools.partial(grad_query_kernel, count, heads),
            "grad_queries",
            info,
            [grad, key_rows, value_rows, low],
            [block, block, block, states],
            [tokens16],
            [block],
            (),
            8.0,
        )[0]
    with jax.named_scope("grad_keys_values"):
        grad_keys, grad_values = call(
            functools.partial(grad_key_value_kernel, count, heads, length),
            "grad_keys_values",
            info,
            [grad, queries, key_rows, value_rows, after, out_of],
            [block, block, block, block, states, state],
            [tokens16, tokens16],
            [block, block],
            (),
            8.0,
        )
    return (grad_queries, grad_keys, grad_values, grad_gate)


def solution(mesh):
    return jax.shard_map(
        body,
        mesh=mesh,
        in_specs=(
            P(("seq", "head"), None),
            P("head", None),
            P("seq", "head"),
            P("seq", "head"),
            P("seq", "head"),
            P("seq", "head"),
            P(),
        ),
        out_specs=(P("seq", "head"), P("seq", "head"), P("seq", "head"), P("seq", "head")),
        check_vma=False,
    )
```

```python
import functools

import jax
import jax.numpy as jnp
from jax import lax
from jax.experimental import pallas as pl
from jax.experimental.pallas import tpu as pltpu
from jax.sharding import PartitionSpec as P

HEAD_DIM = 128
BLK = 512
CHUNK = 256
EPS = 1e-06
F32 = jnp.float32
BF16 = jnp.bfloat16
VMEM_LIMIT = 16 * 1024 * 1024
PROJECT_VMEM = 16 * 1024 * 1024
PIECES = 2
COST_SCALE = 1.15e9


def dot(a, b):
    return lax.dot_general(a, b, (((1,), (0,)), ((), ())), preferred_element_type=F32)


def dot_nt(a, b):
    return lax.dot_general(a, b, (((1,), (1,)), ((), ())), preferred_element_type=F32)


def dot_tn(a, b):
    return lax.dot_general(a, b, (((0,), (0,)), ((), ())), preferred_element_type=F32)


def doc_of(info, count, pos):
    total = jnp.zeros_like(pos)
    for i in range(count):
        total = total + jnp.where(info[i] <= pos, 1, 0)
    return total


def same(a, b):
    return jnp.where(a == b, F32(1.0), F32(0.0))


def column_docs(info, count, start, size):
    return doc_of(info, count, start + lax.broadcasted_iota(jnp.int32, (size, 1), 0))


def row_docs(info, count, start, size):
    return doc_of(info, count, start + lax.broadcasted_iota(jnp.int32, (1, size), 1))


def causal_mask(info, count, start, transposed):
    down = lax.broadcasted_iota(jnp.int32, (CHUNK, CHUNK), 0)
    over = lax.broadcasted_iota(jnp.int32, (CHUNK, CHUNK), 1)
    equal = column_docs(info, count, start, CHUNK) == row_docs(info, count, start, CHUNK)
    return equal & ((down <= over) if transposed else (over <= down))


def chunk_rows(r):
    return slice(r * CHUNK, (r + 1) * CHUNK)


def lane_sums(x):
    return jnp.sum(x.T, axis=0, keepdims=True)


def to_columns(row):
    return jnp.broadcast_to(row, (HEAD_DIM, row.shape[1])).T


def head_slice(h):
    return slice(h * HEAD_DIM, (h + 1) * HEAD_DIM)


def key_state_kernel(count, heads, info, k_ref, v_ref, before_ref, total_ref, state):
    b = pl.program_id(0)

    @pl.when(b == 0)
    def _():
        state[...] = jnp.zeros_like(state)

    for r in range(BLK // CHUNK):
        rows = chunk_rows(r)
        start = info[count] + b * BLK + r * CHUNK
        last_doc = doc_of(info, count, start + CHUNK - 1)
        keep_out = same(column_docs(info, count, start, CHUNK), last_doc).astype(BF16)
        carry = same(doc_of(info, count, start - 1), last_doc)
        for h in range(heads):
            at = head_slice(h)
            before_ref[r, h] = state[h]
            state[h] = dot_tn(k_ref[rows, at] * keep_out, v_ref[rows, at]) + carry * state[h]
    total_ref[...] = state[...]


def attention_kernel(
    count, heads, info, q_ref, k_ref, v_ref, before_ref, into_ref, attn_ref, square_ref, low_ref
):
    first = info[count]
    for r in range(BLK // CHUNK):
        rows = chunk_rows(r)
        start = first + pl.program_id(0) * BLK + r * CHUNK
        prior = doc_of(info, count, start - 1)
        carry = same(prior, doc_of(info, count, first - 1))
        mask = causal_mask(info, count, start, False)
        keep_in = same(column_docs(info, count, start, CHUNK), prior)
        squares = jnp.zeros((CHUNK, HEAD_DIM), F32)
        for h in range(heads):
            at = head_slice(h)
            low = (before_ref[r, h] + carry * into_ref[h]).astype(BF16)
            low_ref[r, h] = low
            q = q_ref[rows, at]
            probs = jnp.where(mask, dot_nt(q, k_ref[rows, at]), 0.0).astype(BF16)
            out = keep_in * dot(q, low) + dot(probs, v_ref[rows, at])
            attn_ref[rows, at] = out
            squares = squares + out * out
        square_ref[:, rows] = lane_sums(squares)


def mix_heads(heads, info, near_ref, far_ref):
    core = info[info.shape[0] - 1]
    half = heads // 2
    for index, ref in enumerate((near_ref, far_ref)):
        for i in range(half):
            h = (core ^ index) * half + i
            at = pl.ds(pl.multiple_of(h * HEAD_DIM, HEAD_DIM), HEAD_DIM)
            yield ref.at[:, head_slice(i)], at


def cross_kernel(heads, info, near_ref, far_ref, gate_ref, attn_ref, square_ref, sums_ref):
    total = jnp.zeros((BLK, HEAD_DIM), F32)
    for mix, at in mix_heads(heads, info, near_ref, far_ref):
        total = total + mix[...].astype(F32) * gate_ref[:, at].astype(F32) * attn_ref[:, at]
    sums_ref[0:1, :] = square_ref[...]
    sums_ref[1:2, :] = lane_sums(total)


def grad_attn_kernel(
    count,
    heads,
    width,
    info,
    near_ref,
    far_ref,
    gate_ref,
    attn_ref,
    q_ref,
    sums_ref,
    grad_ref,
    gate_grad_ref,
    after_ref,
    total_ref,
    low_ref,
    state,
):
    @pl.when(pl.program_id(0) == 0)
    def _():
        state[...] = jnp.zeros_like(state)

    b = pl.num_programs(0) - 1 - pl.program_id(0)
    rms = jnp.sqrt(sums_ref[0:1, :] / width + EPS)
    inverse = to_columns(1.0 / rms)
    pull = to_columns(sums_ref[1:2, :] / (width * (rms * rms * rms)))
    for r in reversed(range(BLK // CHUNK)):
        rows = chunk_rows(r)
        start = info[count] + b * BLK + r * CHUNK
        prior = doc_of(info, count, start - 1)
        keep_in = same(column_docs(info, count, start, CHUNK), prior).astype(BF16)
        carry = same(doc_of(info, count, start + CHUNK - 1), prior)
        half = heads // 2
        for i, (mix, at) in enumerate(mix_heads(heads, info, near_ref, far_ref)):
            h = (info[count + 1] ^ (i // half)) * half + i % half
            scaled = mix[rows].astype(F32) * inverse[rows]
            attn = attn_ref[rows, at]
            gate_grad_ref[rows, at] = (scaled * attn).astype(BF16)
            grad = (scaled * gate_ref[rows, at].astype(F32) - attn * pull[rows]).astype(BF16)
            grad_ref[rows, at] = grad
            after_ref[r, h] = state[h]
            state[h] = dot_tn(q_ref[rows, at] * keep_in, grad) + carry * state[h]
    total_ref[...] = state[...]
    low_ref[...] = state[...].astype(BF16)


def grad_query_kernel(count, heads, info, grad_ref, k_ref, v_ref, low_ref, out_ref):
    for r in range(BLK // CHUNK):
        rows = chunk_rows(r)
        start = info[count] + pl.program_id(0) * BLK + r * CHUNK
        prior = doc_of(info, count, start - 1)
        mask = causal_mask(info, count, start, False)
        keep_in = same(column_docs(info, count, start, CHUNK), prior)
        for h in range(heads):
            at = head_slice(h)
            grad = grad_ref[rows, at]
            dprob = jnp.where(mask, dot_nt(grad, v_ref[rows, at]), 0.0).astype(BF16)
            out = keep_in * dot_nt(grad, low_ref[r, h]) + dot(dprob, k_ref[rows, at])
            out_ref[rows, at] = out.astype(BF16)


def grad_key_value_kernel(
    count, heads, length, info, grad_ref, q_ref, k_ref, v_ref, after_ref, *refs
):
    *landed, dk_ref, dv_ref, into_ref = refs
    first = info[count]

    @pl.when(pl.program_id(0) == 0)
    def _():
        place = lax.div(first, length)
        last_doc = doc_of(info, count, first + length - 1)
        total = None
        for index, ref in enumerate(landed):
            source = place ^ (index + 1)
            takes = jnp.where(source > place, F32(1.0), F32(0.0))
            takes = takes * same(doc_of(info, count, source * length - 1), last_doc)
            term = ref[...].astype(F32) * takes
            total = term if total is None else total + term
        into_ref[...] = total

    for r in range(BLK // CHUNK):
        rows = chunk_rows(r)
        start = first + pl.program_id(0) * BLK + r * CHUNK
        last_doc = doc_of(info, count, start + CHUNK - 1)
        carry = same(last_doc, doc_of(info, count, first + length - 1))
        mask = causal_mask(info, count, start, True)
        keep_out = same(column_docs(info, count, start, CHUNK), last_doc)
        for h in range(heads):
            at = head_slice(h)
            low = (after_ref[r, h] + carry * into_ref[h]).astype(BF16)
            k, v, q, grad = k_ref[rows, at], v_ref[rows, at], q_ref[rows, at], grad_ref[rows, at]
            dprob = jnp.where(mask, dot_nt(v, grad), 0.0).astype(BF16)
            probs = jnp.where(mask, dot_nt(k, q), 0.0).astype(BF16)
            dk_ref[rows, at] = (keep_out * dot_nt(v, low) + dot(dprob, q)).astype(BF16)
            dv_ref[rows, at] = (keep_out * dot(k, low) + dot(probs, grad)).astype(BF16)


def combine_kernel(count, length, size, info, total_ref, other_ref, into_ref, *outs):
    first = info[count]
    place = lax.div(first, length)
    group = lax.div(place, size)
    other_doc = doc_of(info, count, ((group ^ 1) + 1) * (size * length) - 1)
    my_doc = doc_of(info, count, (group + 1) * (size * length) - 1)
    later = same(group & 1, 1)
    reaches = later * same(other_doc, doc_of(info, count, first - 1))
    joined = same(other_doc, my_doc)
    total_share = later + (1.0 - later) * joined
    other_share = later * joined + (1.0 - later)
    other = other_ref[...].astype(F32)
    total = total_ref[...].astype(F32) * total_share + other * other_share
    outs[0][...] = total.astype(BF16)
    outs[1][...] = into_ref[...] + other * reaches


def combine(info, count, length, size, total, other, into):
    whole = pl.BlockSpec(total.shape, lambda i, s: (0, 0, 0))
    return pl.pallas_call(
        functools.partial(combine_kernel, count, length, size),
        grid_spec=pltpu.PrefetchScalarGridSpec(
            num_scalar_prefetch=1, grid=(1,), in_specs=[whole] * 3, out_specs=[whole] * 2
        ),
        out_shape=[
            jax.ShapeDtypeStruct(total.shape, BF16),
            jax.ShapeDtypeStruct(total.shape, F32),
        ],
        name="combine",
        cost_estimate=cost(1.0),
        compiler_params=pltpu.CompilerParams(vmem_limit_bytes=VMEM_LIMIT),
    )(info, total, other, into)


def gather_kernel(info, *refs):
    sets, out, arrived = refs[:4], refs[4], refs[5]
    rows = sets[0].shape[0]
    copies = []
    for index, ref in enumerate(sets):
        place = 2 * (info[2] ^ (index // 2)) + (info[0] ^ (index % 2))
        at = pl.ds(pl.multiple_of(place * rows, rows), rows)
        copies.append(pltpu.make_async_copy(ref, out.at[at, :], arrived.at[index]))
    for copy in copies:
        copy.start()
    for copy in copies:
        copy.wait()


def gather_rows(info, sets):
    rows, depth = sets[0].shape
    return pl.pallas_call(
        gather_kernel,
        grid_spec=pltpu.PrefetchScalarGridSpec(
            num_scalar_prefetch=1,
            grid=(1,),
            in_specs=[pl.BlockSpec(memory_space=pl.ANY)] * 4,
            out_specs=pl.BlockSpec(memory_space=pltpu.VMEM),
            scratch_shapes=[pltpu.SemaphoreType.DMA((4,))],
        ),
        out_shape=jax.ShapeDtypeStruct((4 * rows, depth), BF16),
        name="gather_rows",
        cost_estimate=cost(3.0),
        compiler_params=pltpu.CompilerParams(vmem_limit_bytes=PROJECT_VMEM),
    )(info, *sets)


def project_kernel(split, info, rows_ref, *refs):
    count = len(refs) // (split + 1)
    shards, outs = refs[: count * split], refs[count * split :]
    part = rows_ref.shape[1] // split
    total = None
    for j in range(split):
        if split == 1:
            left = rows_ref[...]
        else:
            left = rows_ref[:, pl.ds(pl.multiple_of((info[1] ^ j) * part, part), part)]
        weights = [shards[i * split + j][...] for i in range(count)]
        weights = weights[0] if count == 1 else jnp.concatenate(weights, axis=0)
        term = dot_nt(left, weights)
        total = term if total is None else total + term
    width = total.shape[1] // count
    for i, out in enumerate(outs):
        out[...] = total[:, i * width : (i + 1) * width].astype(BF16)


def project(info, rows, shards):
    args = [rows, *(part for parts in shards for part in parts)]
    outs = [jax.ShapeDtypeStruct((rows.shape[0], shards[0][0].shape[0]), BF16)] * len(shards)
    return pl.pallas_call(
        functools.partial(project_kernel, len(shards[0])),
        grid_spec=pltpu.PrefetchScalarGridSpec(
            num_scalar_prefetch=1,
            grid=(1,),
            in_specs=[pl.BlockSpec(memory_space=pltpu.VMEM) for a in args],
            out_specs=[pl.BlockSpec(memory_space=pltpu.VMEM) for o in outs],
        ),
        out_shape=outs,
        name="project",
        cost_estimate=cost(3.0),
        compiler_params=pltpu.CompilerParams(vmem_limit_bytes=PROJECT_VMEM),
    )(info, *args)


def add_kernel(*refs):
    total = refs[0][...]
    for ref in refs[1:-1]:
        total = total + ref[...]
    refs[-1][...] = total


def add_all(arrays):
    return pl.pallas_call(
        add_kernel,
        in_specs=[pl.BlockSpec(memory_space=pltpu.VMEM)] * len(arrays),
        out_specs=pl.BlockSpec(memory_space=pltpu.VMEM),
        out_shape=jax.ShapeDtypeStruct(arrays[0].shape, arrays[0].dtype),
        name="add_all",
        cost_estimate=cost(0.7),
        compiler_params=pltpu.CompilerParams(vmem_limit_bytes=2 * 1024 * 1024),
    )(*arrays)


def cost(micros):
    return pl.CostEstimate(
        flops=int(micros * COST_SCALE), bytes_accessed=0, transcendentals=0
    )


def grad_mixture(out_grad, out_weight, length, early, middle, late):
    n_head = lax.axis_size("head")
    n_pairs = n_head // 2
    rows, depth = out_grad.shape
    width = out_weight.shape[0]
    half = width // 2
    piece_size = half // PIECES
    part_depth = depth // 2
    me = lax.axis_index("head")
    side, pair = me % 2, me // 2
    core = lax.axis_index("seq") % 2
    slot = (lax.axis_index("seq") // 2) % 2
    info = jnp.stack([side, slot, core]).astype(jnp.int32)
    pair, core, slot = (value.astype(jnp.uint32) for value in (pair, core, slot))
    nothing = jnp.uint32(0)
    hops = sorted(range(1, n_pairs), key=lambda k: (bin(k).count("1"), -k))
    order = [(0, hop) for hop in hops if hop & (hop - 1) == 0]
    order += [(1, hop) for hop in hops[:1]]
    order += [(0, hop) for hop in hops if hop & (hop - 1) != 0]
    order += [(1, hop) for hop in hops[1:]]
    waves = [order[i : i + 2] for i in range(0, len(order), 2)]

    fetched = {
        (piece, 0): lax.dynamic_slice(
            out_weight,
            (core * half + jnp.uint32(piece * piece_size), slot * part_depth),
            (piece_size, part_depth),
        )
        for piece in range(PIECES)
    }
    rows_after, _ = lax.optimization_barrier((out_grad, fetched[0, 0]))
    sets = [out_grad, flip(rows_after, "head", 1), None, None]
    across = {}
    arrived = {}
    for step in range(len(waves) + 2):
        wave = waves[step] if step < len(waves) else []
        landed = waves[step - 1] if 0 < step <= len(waves) else []
        spread = waves[step - 2] if 1 < step else []
        for piece, hop in wave:
            low = hop & -hop
            fetched[piece, hop] = flip(fetched[piece, hop ^ low], "head", 2 * low)
        for key in landed:
            across[key] = flip(fetched[key], "seq", 2)
        made = []
        if step == 0:
            sets[2] = flip(rows_after, "seq", 1)
            made.append(sets[2])
        if step == 1:
            weight, _ = lax.optimization_barrier((out_weight, fetched[waves[0][0]]))
            mine = lax.dynamic_slice(weight, (core * half, nothing), (half, depth))
            made += [mine, sets[1], early(fetched[waves[0][0]])]
        if step == 2:
            sets[3] = flip(sets[1], "seq", 1)
            all_rows = gather_rows(info, sets)
        if spread:
            shards = [[fetched[key], across[key]] for key in spread]
            products = project(info, all_rows, shards)
            made += products
            for key, product in zip(spread, products):
                arrived[key] = flip(product, "head", 2 * key[1])
        if step >= 2 and size < lax.axis_size("seq"):
            total, _ = lax.optimization_barrier((total, products[0]))
            total, into = middle(total, into, size)
            size *= 2
        if step == len(waves) + 1:
            while size < lax.axis_size("seq"):
                total, into = middle(total, into, size)
                size *= 2
            attended = late(products[0], into)
        if step == 3:
            arrived[0, 0] = project(info, all_rows, [[mine]])[0]
            made.append(arrived[0, 0])
        if step < len(waves) + 1:
            names = [key for key in fetched if key not in wave]
            carried = (total, into) if step > 1 else ()
            keep, new, far, made, carried = lax.optimization_barrier(
                (
                    [fetched[key] for key in names],
                    [fetched[key] for key in wave],
                    [across[key] for key in landed],
                    made,
                    carried,
                )
            )
            if step == 0:
                sets[2] = made[0]
            if step == 1:
                mine, sets[1], total = made
                into, size = jnp.zeros_like(total), 1
            elif step > 1:
                total, into = carried
            fetched.update(zip(names, keep))
            fetched.update(zip(wave, new))
            across.update(zip(landed, far))
    last = [arrived[key] for key in spread]
    last, _ = lax.optimization_barrier((last, attended))
    arrived.update(zip(spread, last))
    mixes = []
    for source in (None, 1):
        mix = jnp.zeros((length, half), BF16)
        for (piece, hop), product in arrived.items():
            which = core if source is None else jnp.uint32(1) - core
            product = lax.dynamic_slice(
                product, (which * (2 * rows), nothing), (2 * rows, product.shape[1])
            )
            mix = lax.dynamic_update_slice(
                mix, product, ((pair ^ jnp.uint32(hop)) * (2 * rows), jnp.uint32(piece * piece_size))
            )
        mixes.append(mix)
    return mixes[0], flip(mixes[1], "seq", 1)


def call(kernel, name, info, args, in_specs, outs, out_specs, scratch=(), micros=3.0):
    nblocks = max(a.shape[0] for a in args if a.ndim == 2) // BLK
    return pl.pallas_call(
        kernel,
        grid_spec=pltpu.PrefetchScalarGridSpec(
            num_scalar_prefetch=1,
            grid=(nblocks,),
            in_specs=in_specs,
            out_specs=out_specs,
            scratch_shapes=list(scratch),
        ),
        out_shape=outs,
        name=name,
        cost_estimate=cost(micros),
        compiler_params=pltpu.CompilerParams(vmem_limit_bytes=VMEM_LIMIT),
    )(info, *args)


def shaped(shape, dtype):
    return jax.ShapeDtypeStruct(shape, dtype)


def flip(a, axis, bit):
    return lax.ppermute(a, axis, [(i, i ^ bit) for i in range(lax.axis_size(axis))])


def subsets(items):
    found = [[]]
    for item in items:
        found += [[*one, item] for one in found]
    return found[1:]


def head_sum(sums):
    bits = [1 << i for i in range(lax.axis_size("head").bit_length() - 1)]
    for group in (bits[1:3], bits[:1], bits[3:]):
        spans = [sum(chosen) for chosen in subsets(group)]
        if spans:
            sums = add_all([sums, *(flip(sums, "head", span) for span in spans)])
    return sums


def body(out_grad, out_weight, queries, key_rows, value_rows, gate_out, doc_starts):
    length, width = queries.shape
    heads = width // HEAD_DIM
    nblocks = length // BLK
    count = doc_starts.shape[0]
    full_width = width * lax.axis_size("head")
    place = lax.axis_index("seq")
    first = place * length
    info = jnp.concatenate([doc_starts, jnp.stack([first, place % 2]).astype(jnp.int32)])

    block = pl.BlockSpec((BLK, width), lambda b, s: (b, 0))
    half_block = pl.BlockSpec((BLK, width // 2), lambda b, s: (b, 0))
    line = pl.BlockSpec((1, BLK), lambda b, s: (0, b))
    states = pl.BlockSpec((BLK // CHUNK, heads, HEAD_DIM, HEAD_DIM), lambda b, s: (b, 0, 0, 0))
    state = pl.BlockSpec((heads, HEAD_DIM, HEAD_DIM), lambda b, s: (0, 0, 0))
    one_state = shaped((heads, HEAD_DIM, HEAD_DIM), F32)
    low_state = shaped((heads, HEAD_DIM, HEAD_DIM), BF16)
    all_states = shaped((length // CHUNK, heads, HEAD_DIM, HEAD_DIM), F32)
    low_states = shaped((length // CHUNK, heads, HEAD_DIM, HEAD_DIM), BF16)
    tokens16 = shaped((length, width), BF16)
    tokens32 = shaped((length, width), F32)
    row = shaped((1, length), F32)
    scratch = [pltpu.VMEM((heads, HEAD_DIM, HEAD_DIM), F32)]

    kept = {}

    def early(landed):
        keys, values, _ = lax.optimization_barrier((key_rows, value_rows, landed))
        with jax.named_scope("key_states"):
            before, key_total = call(
                functools.partial(key_state_kernel, count, heads),
                "key_states",
                info,
                [keys, values],
                [block, block],
                [all_states, one_state],
                [states, state],
                scratch,
            )
        kept["before"] = before
        return key_total

    def middle(total, into, size):
        return combine(info, count, length, size, total, flip(total, "seq", size), into)

    def late(product, into):
        kept["into"] = into
        tokens, _ = lax.optimization_barrier((queries, product))
        with jax.named_scope("attention"):
            kept["attn"], kept["square"], kept["low"] = call(
                functools.partial(attention_kernel, count, heads),
                "attention",
                info,
                [tokens, key_rows, value_rows, kept["before"], kept["into"]],
                [block, block, block, states, state],
                [tokens32, row, low_states],
                [block, line, states],
            )
        return kept["square"]

    near, far = grad_mixture(out_grad, out_weight, length, early, middle, late)
    attn, square, low = kept["attn"], kept["square"], kept["low"]

    with jax.named_scope("cross"):
        sums = call(
            functools.partial(cross_kernel, heads),
            "cross",
            info,
            [near, far, gate_out, attn, square],
            [half_block, half_block, block, block, line],
            [shaped((2, length), F32)],
            [pl.BlockSpec((2, BLK), lambda b, s: (0, b))],
        )[0]

    sums = head_sum(sums)

    back = lambda spec_shape, f: pl.BlockSpec(spec_shape, lambda b, s: f(nblocks - 1 - b))
    block_r = back((BLK, width), lambda b: (b, 0))
    half_r = back((BLK, width // 2), lambda b: (b, 0))
    line_r = back((2, BLK), lambda b: (0, b))
    states_r = back((BLK // CHUNK, heads, HEAD_DIM, HEAD_DIM), lambda b: (b, 0, 0, 0))
    with jax.named_scope("grad_attn"):
        grad, grad_gate, after, query_total, query_low = call(
            functools.partial(grad_attn_kernel, count, heads, full_width),
            "grad_attn",
            info,
            [near, far, gate_out, attn, queries, sums],
            [half_r, half_r, block_r, block_r, block_r, line_r],
            [tokens16, tokens16, all_states, one_state, low_state],
            [block_r, block_r, states_r, state, state],
            scratch,
            4.0,
        )
    landed = [
        flip(query_total if step == 1 else query_low, "seq", step)
        for step in range(1, lax.axis_size("seq"))
    ]
    with jax.named_scope("grad_queries"):
        grad_queries = call(
            functools.partial(grad_query_kernel, count, heads),
            "grad_queries",
            info,
            [grad, key_rows, value_rows, low],
            [block, block, block, states],
            [tokens16],
            [block],
            (),
            8.0,
        )[0]
    with jax.named_scope("grad_keys_values"):
        grad_keys, grad_values = call(
            functools.partial(grad_key_value_kernel, count, heads, length),
            "grad_keys_values",
            info,
            [grad, queries, key_rows, value_rows, after, *landed],
            [block, block, block, block, states] + [state] * len(landed),
            [tokens16, tokens16],
            [block, block],
            scratch,
            8.0,
        )
    return (grad_queries, grad_keys, grad_values, grad_gate)


def solution(mesh):
    return jax.shard_map(
        body,
        mesh=mesh,
        in_specs=(
            P(("seq", "head"), None),
            P("head", None),
            P("seq", "head"),
            P("seq", "head"),
            P("seq", "head"),
            P("seq", "head"),
            P(),
        ),
        out_specs=(P("seq", "head"), P("seq", "head"), P("seq", "head"), P("seq", "head")),
        check_vma=False,
    )
```

```python
import functools

import jax
import jax.numpy as jnp
from jax import lax
from jax.experimental import pallas as pl
from jax.experimental.pallas import tpu as pltpu
from jax.sharding import PartitionSpec as P

HEAD_DIM = 128
BLK = 512
LARGE = 1024
CHUNK = 256
EPS = 1e-06
F32 = jnp.float32
BF16 = jnp.bfloat16
VMEM_LIMIT = 16 * 1024 * 1024
PROJECT_VMEM = 16 * 1024 * 1024
PIECES = 2
COST_SCALE = 1.15e9


def dot(a, b):
    return lax.dot_general(a, b, (((1,), (0,)), ((), ())), preferred_element_type=F32)


def dot_nt(a, b):
    return lax.dot_general(a, b, (((1,), (1,)), ((), ())), preferred_element_type=F32)


def dot_tn(a, b):
    return lax.dot_general(a, b, (((0,), (0,)), ((), ())), preferred_element_type=F32)


def doc_of(info, count, pos):
    total = jnp.zeros_like(pos)
    for i in range(count):
        total = total + jnp.where(info[i] <= pos, 1, 0)
    return total


def same(a, b):
    return jnp.where(a == b, F32(1.0), F32(0.0))


def column_docs(info, count, start, size):
    return doc_of(info, count, start + lax.broadcasted_iota(jnp.int32, (size, 1), 0))


def row_docs(info, count, start, size):
    return doc_of(info, count, start + lax.broadcasted_iota(jnp.int32, (1, size), 1))


def causal_mask(info, count, start, transposed):
    down = lax.broadcasted_iota(jnp.int32, (CHUNK, CHUNK), 0)
    over = lax.broadcasted_iota(jnp.int32, (CHUNK, CHUNK), 1)
    equal = column_docs(info, count, start, CHUNK) == row_docs(info, count, start, CHUNK)
    return equal & ((down <= over) if transposed else (over <= down))


def chunk_rows(r):
    return slice(r * CHUNK, (r + 1) * CHUNK)


def lane_sums(x):
    return jnp.sum(x.T, axis=0, keepdims=True)


def to_columns(row):
    return jnp.broadcast_to(row, (HEAD_DIM, row.shape[1])).T


def head_slice(h):
    return slice(h * HEAD_DIM, (h + 1) * HEAD_DIM)


def key_state_kernel(count, heads, info, k_ref, v_ref, before_ref, total_ref, state):
    b = pl.program_id(0)

    @pl.when(b == 0)
    def _():
        state[...] = jnp.zeros_like(state)

    for r in range(BLK // CHUNK):
        rows = chunk_rows(r)
        start = info[count] + b * BLK + r * CHUNK
        last_doc = doc_of(info, count, start + CHUNK - 1)
        keep_out = same(column_docs(info, count, start, CHUNK), last_doc).astype(BF16)
        carry = same(doc_of(info, count, start - 1), last_doc)
        for h in range(heads):
            at = head_slice(h)
            before_ref[r, h] = state[h]
            state[h] = dot_tn(k_ref[rows, at] * keep_out, v_ref[rows, at]) + carry * state[h]
    total_ref[...] = state[...]


def attention_kernel(
    count, heads, info, q_ref, k_ref, v_ref, before_ref, into_ref, attn_ref, square_ref, low_ref
):
    first = info[count]
    size = q_ref.shape[0]
    for r in range(size // CHUNK):
        rows = chunk_rows(r)
        start = first + pl.program_id(0) * size + r * CHUNK
        prior = doc_of(info, count, start - 1)
        carry = same(prior, doc_of(info, count, first - 1))
        mask = causal_mask(info, count, start, False)
        keep_in = same(column_docs(info, count, start, CHUNK), prior)
        probs, carried = [], []
        for h in range(heads):
            at = head_slice(h)
            low = (before_ref[r, h] + carry * into_ref[h]).astype(BF16)
            low_ref[r, h] = low
            q = q_ref[rows, at]
            probs.append(jnp.where(mask, dot_nt(q, k_ref[rows, at]), 0.0).astype(BF16))
            carried.append(keep_in * dot(q, low))
        squares = jnp.zeros((CHUNK, HEAD_DIM), F32)
        for h in range(heads):
            at = head_slice(h)
            out = carried[h] + dot(probs[h], v_ref[rows, at])
            attn_ref[rows, at] = out
            squares = squares + out * out
        square_ref[:, rows] = lane_sums(squares)


def mix_heads(heads, info, near_ref, far_ref):
    core = info[info.shape[0] - 1]
    half = heads // 2
    for index, ref in enumerate((near_ref, far_ref)):
        for i in range(half):
            h = (core ^ index) * half + i
            at = pl.ds(pl.multiple_of(h * HEAD_DIM, HEAD_DIM), HEAD_DIM)
            yield ref.at[:, head_slice(i)], at


def cross_kernel(heads, info, near_ref, far_ref, gate_ref, attn_ref, square_ref, sums_ref):
    total = jnp.zeros((BLK, HEAD_DIM), F32)
    for mix, at in mix_heads(heads, info, near_ref, far_ref):
        total = total + mix[...].astype(F32) * gate_ref[:, at].astype(F32) * attn_ref[:, at]
    sums_ref[0:1, :] = square_ref[...]
    sums_ref[1:2, :] = lane_sums(total)


def grad_attn_kernel(
    count,
    heads,
    width,
    info,
    near_ref,
    far_ref,
    gate_ref,
    attn_ref,
    q_ref,
    sums_ref,
    grad_ref,
    gate_grad_ref,
    after_ref,
    total_ref,
    low_ref,
    state,
):
    @pl.when(pl.program_id(0) == 0)
    def _():
        state[...] = jnp.zeros_like(state)

    b = pl.num_programs(0) - 1 - pl.program_id(0)
    rms = jnp.sqrt(sums_ref[0:1, :] / width + EPS)
    inverse = to_columns(1.0 / rms)
    pull = to_columns(sums_ref[1:2, :] / (width * (rms * rms * rms)))
    for r in reversed(range(BLK // CHUNK)):
        rows = chunk_rows(r)
        start = info[count] + b * BLK + r * CHUNK
        prior = doc_of(info, count, start - 1)
        keep_in = same(column_docs(info, count, start, CHUNK), prior).astype(BF16)
        carry = same(doc_of(info, count, start + CHUNK - 1), prior)
        half = heads // 2
        for i, (mix, at) in enumerate(mix_heads(heads, info, near_ref, far_ref)):
            h = (info[count + 1] ^ (i // half)) * half + i % half
            scaled = mix[rows].astype(F32) * inverse[rows]
            attn = attn_ref[rows, at]
            gate_grad_ref[rows, at] = (scaled * attn).astype(BF16)
            grad = (scaled * gate_ref[rows, at].astype(F32) - attn * pull[rows]).astype(BF16)
            grad_ref[rows, at] = grad
            after_ref[r, h] = state[h]
            state[h] = dot_tn(q_ref[rows, at] * keep_in, grad) + carry * state[h]
    total_ref[...] = state[...]
    low_ref[...] = state[...].astype(BF16)


def grad_query_kernel(count, heads, info, grad_ref, k_ref, v_ref, low_ref, out_ref):
    size = grad_ref.shape[0]
    for r in range(size // CHUNK):
        rows = chunk_rows(r)
        start = info[count] + pl.program_id(0) * size + r * CHUNK
        prior = doc_of(info, count, start - 1)
        mask = causal_mask(info, count, start, False)
        keep_in = same(column_docs(info, count, start, CHUNK), prior)
        dprobs, carried = [], []
        for h in range(heads):
            at = head_slice(h)
            grad = grad_ref[rows, at]
            dprobs.append(jnp.where(mask, dot_nt(grad, v_ref[rows, at]), 0.0).astype(BF16))
            carried.append(keep_in * dot_nt(grad, low_ref[r, h]))
        for h in range(heads):
            at = head_slice(h)
            out_ref[rows, at] = (carried[h] + dot(dprobs[h], k_ref[rows, at])).astype(BF16)


def grad_key_value_kernel(
    count, heads, length, info, grad_ref, q_ref, k_ref, v_ref, after_ref, *refs
):
    *landed, dk_ref, dv_ref, into_ref = refs
    first = info[count]
    size = grad_ref.shape[0]

    @pl.when(pl.program_id(0) == 0)
    def _():
        place = lax.div(first, length)
        last_doc = doc_of(info, count, first + length - 1)
        total = None
        for index, ref in enumerate(landed):
            source = place ^ (index + 1)
            takes = jnp.where(source > place, F32(1.0), F32(0.0))
            takes = takes * same(doc_of(info, count, source * length - 1), last_doc)
            term = ref[...].astype(F32) * takes
            total = term if total is None else total + term
        into_ref[...] = total

    for r in range(size // CHUNK):
        rows = chunk_rows(r)
        start = first + pl.program_id(0) * size + r * CHUNK
        last_doc = doc_of(info, count, start + CHUNK - 1)
        carry = same(last_doc, doc_of(info, count, first + length - 1))
        mask = causal_mask(info, count, start, True)
        keep_out = same(column_docs(info, count, start, CHUNK), last_doc)
        for pair in range(0, heads, 2):
            parts = []
            for h in range(pair, min(pair + 2, heads)):
                at = head_slice(h)
                low = (after_ref[r, h] + carry * into_ref[h]).astype(BF16)
                k, v = k_ref[rows, at], v_ref[rows, at]
                dprob = jnp.where(mask, dot_nt(v, grad_ref[rows, at]), 0.0).astype(BF16)
                probs = jnp.where(mask, dot_nt(k, q_ref[rows, at]), 0.0).astype(BF16)
                parts.append(
                    (at, dprob, probs, keep_out * dot_nt(v, low), keep_out * dot(k, low))
                )
            for at, dprob, probs, from_v, from_k in parts:
                dk_ref[rows, at] = (from_v + dot(dprob, q_ref[rows, at])).astype(BF16)
                dv_ref[rows, at] = (from_k + dot(probs, grad_ref[rows, at])).astype(BF16)


def combine_kernel(count, length, size, info, total_ref, other_ref, into_ref, *outs):
    first = info[count]
    place = lax.div(first, length)
    group = lax.div(place, size)
    other_doc = doc_of(info, count, ((group ^ 1) + 1) * (size * length) - 1)
    my_doc = doc_of(info, count, (group + 1) * (size * length) - 1)
    later = same(group & 1, 1)
    reaches = later * same(other_doc, doc_of(info, count, first - 1))
    joined = same(other_doc, my_doc)
    total_share = later + (1.0 - later) * joined
    other_share = later * joined + (1.0 - later)
    other = other_ref[...].astype(F32)
    total = total_ref[...].astype(F32) * total_share + other * other_share
    outs[0][...] = total.astype(BF16)
    outs[1][...] = into_ref[...] + other * reaches


def combine(info, count, length, size, total, other, into):
    whole = pl.BlockSpec(total.shape, lambda i, s: (0, 0, 0))
    return pl.pallas_call(
        functools.partial(combine_kernel, count, length, size),
        grid_spec=pltpu.PrefetchScalarGridSpec(
            num_scalar_prefetch=1, grid=(1,), in_specs=[whole] * 3, out_specs=[whole] * 2
        ),
        out_shape=[
            jax.ShapeDtypeStruct(total.shape, BF16),
            jax.ShapeDtypeStruct(total.shape, F32),
        ],
        name="combine",
        cost_estimate=cost(1.0),
        compiler_params=pltpu.CompilerParams(vmem_limit_bytes=VMEM_LIMIT),
    )(info, total, other, into)


def gather_kernel(info, *refs):
    sets, out, arrived = refs[:4], refs[4], refs[5]
    rows = sets[0].shape[0]
    copies = []
    for index, ref in enumerate(sets):
        place = 2 * (info[2] ^ (index // 2)) + (info[0] ^ (index % 2))
        at = pl.ds(pl.multiple_of(place * rows, rows), rows)
        copies.append(pltpu.make_async_copy(ref, out.at[at, :], arrived.at[index]))
    for copy in copies:
        copy.start()
    for copy in copies:
        copy.wait()


def gather_rows(info, sets):
    rows, depth = sets[0].shape
    return pl.pallas_call(
        gather_kernel,
        grid_spec=pltpu.PrefetchScalarGridSpec(
            num_scalar_prefetch=1,
            grid=(1,),
            in_specs=[pl.BlockSpec(memory_space=pl.ANY)] * 4,
            out_specs=pl.BlockSpec(memory_space=pltpu.VMEM),
            scratch_shapes=[pltpu.SemaphoreType.DMA((4,))],
        ),
        out_shape=jax.ShapeDtypeStruct((4 * rows, depth), BF16),
        name="gather_rows",
        cost_estimate=cost(3.0),
        compiler_params=pltpu.CompilerParams(vmem_limit_bytes=PROJECT_VMEM),
    )(info, *sets)


def project_kernel(split, info, rows_ref, *refs):
    count = len(refs) // (split + 1)
    shards, outs = refs[: count * split], refs[count * split :]
    part = rows_ref.shape[1] // split
    total = None
    for j in range(split):
        if split == 1:
            left = rows_ref[...]
        else:
            left = rows_ref[:, pl.ds(pl.multiple_of((info[1] ^ j) * part, part), part)]
        weights = [shards[i * split + j][...] for i in range(count)]
        weights = weights[0] if count == 1 else jnp.concatenate(weights, axis=0)
        term = dot_nt(left, weights)
        total = term if total is None else total + term
    width = total.shape[1] // count
    for i, out in enumerate(outs):
        out[...] = total[:, i * width : (i + 1) * width].astype(BF16)


def project(info, rows, shards):
    args = [rows, *(part for parts in shards for part in parts)]
    outs = [jax.ShapeDtypeStruct((rows.shape[0], shards[0][0].shape[0]), BF16)] * len(shards)
    return pl.pallas_call(
        functools.partial(project_kernel, len(shards[0])),
        grid_spec=pltpu.PrefetchScalarGridSpec(
            num_scalar_prefetch=1,
            grid=(1,),
            in_specs=[pl.BlockSpec(memory_space=pltpu.VMEM)]
            * len(args),
            out_specs=[pl.BlockSpec(memory_space=pltpu.VMEM) for o in outs],
        ),
        out_shape=outs,
        name="project",
        cost_estimate=cost(3.0),
        compiler_params=pltpu.CompilerParams(vmem_limit_bytes=PROJECT_VMEM),
    )(info, *args)


def add_kernel(*refs):
    total = refs[0][...]
    for ref in refs[1:-1]:
        total = total + ref[...]
    refs[-1][...] = total


def add_all(arrays):
    return pl.pallas_call(
        add_kernel,
        in_specs=[pl.BlockSpec(memory_space=pltpu.VMEM)] * len(arrays),
        out_specs=pl.BlockSpec(memory_space=pltpu.VMEM),
        out_shape=jax.ShapeDtypeStruct(arrays[0].shape, arrays[0].dtype),
        name="add_all",
        cost_estimate=cost(0.7),
        compiler_params=pltpu.CompilerParams(vmem_limit_bytes=2 * 1024 * 1024),
    )(*arrays)


def cost(micros):
    return pl.CostEstimate(
        flops=int(micros * COST_SCALE), bytes_accessed=0, transcendentals=0
    )


def grad_mixture(out_grad, out_weight, length, early, middle, late):
    n_head = lax.axis_size("head")
    n_pairs = n_head // 2
    rows, depth = out_grad.shape
    width = out_weight.shape[0]
    half = width // 2
    piece_size = half // PIECES
    part_depth = depth // 2
    me = lax.axis_index("head")
    side, pair = me % 2, me // 2
    core = lax.axis_index("seq") % 2
    slot = (lax.axis_index("seq") // 2) % 2
    info = jnp.stack([side, slot, core]).astype(jnp.int32)
    pair, core, slot = (value.astype(jnp.uint32) for value in (pair, core, slot))
    nothing = jnp.uint32(0)
    hops = sorted(range(1, n_pairs), key=lambda k: (bin(k).count("1"), -k))
    order = [(0, hop) for hop in hops if hop & (hop - 1) == 0]
    order += [(1, hop) for hop in hops[:1]]
    order += [(0, hop) for hop in hops if hop & (hop - 1) != 0]
    order += [(1, hop) for hop in hops[1:]]
    order[-2], order[-1] = order[-1], order[-2]
    waves = [order[i : i + 2] for i in range(0, len(order), 2)]

    fetched = {
        (piece, 0): lax.dynamic_slice(
            out_weight,
            (core * half + jnp.uint32(piece * piece_size), slot * part_depth),
            (piece_size, part_depth),
        )
        for piece in range(PIECES)
    }
    rows_after, _ = lax.optimization_barrier((out_grad, fetched[0, 0]))
    sets = [out_grad, flip(rows_after, "head", 1), None, None]
    across = {}
    arrived = {}
    for step in range(len(waves) + 2):
        wave = waves[step] if step < len(waves) else []
        landed = waves[step - 1] if 0 < step <= len(waves) else []
        spread = waves[step - 2] if 1 < step else []
        for piece, hop in wave:
            low = hop & -hop
            fetched[piece, hop] = flip(fetched[piece, hop ^ low], "head", 2 * low)
        for key in landed:
            across[key] = flip(fetched[key], "seq", 2)
        made = []
        if step == 0:
            sets[2] = flip(rows_after, "seq", 1)
            made.append(sets[2])
        if step == 1:
            weight, _ = lax.optimization_barrier((out_weight, fetched[waves[0][0]]))
            mine = lax.dynamic_slice(weight, (core * half, nothing), (half, depth))
            made += [mine, sets[1], early(fetched[waves[0][0]])]
        if step == 2:
            sets[3] = flip(sets[1], "seq", 1)
            all_rows = gather_rows(info, sets)
        last_step = step == len(waves) + 1
        if spread:
            shards = [[fetched[key], across[key]] for key in spread]
            products = project(info, all_rows, shards)
            made += products
            for key, product in zip(spread, products):
                arrived[key] = flip(product, "head", 2 * key[1])
        if step >= 2 and size < lax.axis_size("seq") and (step >= 4 or size == 1):
            total, _ = lax.optimization_barrier((total, products[0]))
            total, into = middle(total, flip(total, "seq", size), into, size)
            size *= 2
        if last_step:
            while size < lax.axis_size("seq"):
                total, into = middle(total, flip(total, "seq", size), into, size)
                size *= 2
            attended = late(products[0], into)
        if step == 3:
            arrived[0, 0] = project(info, all_rows, [[mine]])[0]
            made.append(arrived[0, 0])
        if step < len(waves) + 1:
            names = [key for key in fetched if key not in wave]
            carried = (total, into) if step > 1 else ()
            keep, new, far, made, carried = lax.optimization_barrier(
                (
                    [fetched[key] for key in names],
                    [fetched[key] for key in wave] if step > 0 else [],
                    [across[key] for key in landed],
                    made,
                    carried,
                )
            )
            if step == 0:
                sets[2] = made[0]
            if step == 1:
                mine, sets[1], total = made
                into, size = jnp.zeros_like(total), 1
            elif step > 1:
                total, into = carried
            fetched.update(zip(names, keep))
            if step > 0:
                fetched.update(zip(wave, new))
            across.update(zip(landed, far))
    last = [arrived[key] for key in spread]
    last, _ = lax.optimization_barrier((last, attended))
    arrived.update(zip(spread, last))
    mixes = []
    for source in (None, 1):
        mix = jnp.zeros((length, half), BF16)
        for (piece, hop), product in arrived.items():
            which = core if source is None else jnp.uint32(1) - core
            product = lax.dynamic_slice(
                product, (which * (2 * rows), nothing), (2 * rows, product.shape[1])
            )
            mix = lax.dynamic_update_slice(
                mix, product, ((pair ^ jnp.uint32(hop)) * (2 * rows), jnp.uint32(piece * piece_size))
            )
        mixes.append(mix)
    return mixes[0], flip(mixes[1], "seq", 1)


def call(kernel, name, info, args, in_specs, outs, out_specs, scratch=(), micros=3.0, size=BLK):
    nblocks = max(a.shape[0] for a in args if a.ndim == 2) // size
    return pl.pallas_call(
        kernel,
        grid_spec=pltpu.PrefetchScalarGridSpec(
            num_scalar_prefetch=1,
            grid=(nblocks,),
            in_specs=in_specs,
            out_specs=out_specs,
            scratch_shapes=list(scratch),
        ),
        out_shape=outs,
        name=name,
        cost_estimate=cost(micros),
        compiler_params=pltpu.CompilerParams(vmem_limit_bytes=VMEM_LIMIT),
    )(info, *args)


def shaped(shape, dtype):
    return jax.ShapeDtypeStruct(shape, dtype)


def flip(a, axis, bit):
    return lax.ppermute(a, axis, [(i, i ^ bit) for i in range(lax.axis_size(axis))])


def subsets(items):
    found = [[]]
    for item in items:
        found += [[*one, item] for one in found]
    return found[1:]


def head_sum(sums):
    bits = [1 << i for i in range(lax.axis_size("head").bit_length() - 1)]
    for group in (bits[1:3], bits[:1], bits[3:]):
        spans = [sum(chosen) for chosen in subsets(group)]
        if spans:
            sums = add_all([sums, *(flip(sums, "head", span) for span in spans)])
    return sums


def body(out_grad, out_weight, queries, key_rows, value_rows, gate_out, doc_starts):
    length, width = queries.shape
    heads = width // HEAD_DIM
    nblocks = length // BLK
    count = doc_starts.shape[0]
    full_width = width * lax.axis_size("head")
    place = lax.axis_index("seq")
    first = place * length
    info = jnp.concatenate([doc_starts, jnp.stack([first, place % 2]).astype(jnp.int32)])

    block = pl.BlockSpec((BLK, width), lambda b, s: (b, 0))
    half_block = pl.BlockSpec((BLK, width // 2), lambda b, s: (b, 0))
    line = pl.BlockSpec((1, BLK), lambda b, s: (0, b))
    states = pl.BlockSpec((BLK // CHUNK, heads, HEAD_DIM, HEAD_DIM), lambda b, s: (b, 0, 0, 0))
    state = pl.BlockSpec((heads, HEAD_DIM, HEAD_DIM), lambda b, s: (0, 0, 0))
    one_state = shaped((heads, HEAD_DIM, HEAD_DIM), F32)
    low_state = shaped((heads, HEAD_DIM, HEAD_DIM), BF16)
    all_states = shaped((length // CHUNK, heads, HEAD_DIM, HEAD_DIM), F32)
    low_states = shaped((length // CHUNK, heads, HEAD_DIM, HEAD_DIM), BF16)
    tokens16 = shaped((length, width), BF16)
    tokens32 = shaped((length, width), F32)
    row = shaped((1, length), F32)
    scratch = [pltpu.VMEM((heads, HEAD_DIM, HEAD_DIM), F32)]

    kept = {}

    def early(landed):
        keys, values, _ = lax.optimization_barrier((key_rows, value_rows, landed))
        with jax.named_scope("key_states"):
            before, key_total = call(
                functools.partial(key_state_kernel, count, heads),
                "key_states",
                info,
                [keys, values],
                [block, block],
                [all_states, one_state],
                [states, state],
                scratch,
                3.0,
            )
        kept["before"] = before
        return key_total

    def middle(total, other, into, size):
        return combine(info, count, length, size, total, other, into)

    def late(product, into):
        kept["into"] = into
        tokens, _ = lax.optimization_barrier((queries, product))
        with jax.named_scope("attention"):
            kept["attn"], kept["square"], kept["low"] = call(
                functools.partial(attention_kernel, count, heads),
                "attention",
                info,
                [tokens, key_rows, value_rows, kept["before"], kept["into"]],
                [block, block, block, states, state],
                [tokens32, row, low_states],
                [block, line, states],
                (),
                8.0,
            )
        return kept["square"]

    near, far = grad_mixture(out_grad, out_weight, length, early, middle, late)
    attn, square, low = kept["attn"], kept["square"], kept["low"]

    with jax.named_scope("cross"):
        sums = call(
            functools.partial(cross_kernel, heads),
            "cross",
            info,
            [near, far, gate_out, attn, square],
            [half_block, half_block, block, block, line],
            [shaped((2, length), F32)],
            [pl.BlockSpec((2, BLK), lambda b, s: (0, b))],
        )[0]

    sums = head_sum(sums)

    back = lambda spec_shape, f: pl.BlockSpec(spec_shape, lambda b, s: f(nblocks - 1 - b))
    block_r = back((BLK, width), lambda b: (b, 0))
    half_r = back((BLK, width // 2), lambda b: (b, 0))
    line_r = back((2, BLK), lambda b: (0, b))
    states_r = back((BLK // CHUNK, heads, HEAD_DIM, HEAD_DIM), lambda b: (b, 0, 0, 0))
    with jax.named_scope("grad_attn"):
        grad, grad_gate, after, query_total, query_low = call(
            functools.partial(grad_attn_kernel, count, heads, full_width),
            "grad_attn",
            info,
            [near, far, gate_out, attn, queries, sums],
            [half_r, half_r, block_r, block_r, block_r, line_r],
            [tokens16, tokens16, all_states, one_state, low_state],
            [block_r, block_r, states_r, state, state],
            scratch,
            4.0,
        )
    landed = [
        flip(query_total if step == 1 else query_low, "seq", step)
        for step in range(1, lax.axis_size("seq"))
    ]
    big = pl.BlockSpec((LARGE, width), lambda b, s: (b, 0))
    big_states = pl.BlockSpec(
        (LARGE // CHUNK, heads, HEAD_DIM, HEAD_DIM), lambda b, s: (b, 0, 0, 0)
    )
    with jax.named_scope("grad_queries"):
        grad_queries = call(
            functools.partial(grad_query_kernel, count, heads),
            "grad_queries",
            info,
            [grad, key_rows, value_rows, low],
            [big, big, big, big_states],
            [tokens16],
            [big],
            (),
            8.0,
            LARGE,
        )[0]
    with jax.named_scope("grad_keys_values"):
        grad_keys, grad_values = call(
            functools.partial(grad_key_value_kernel, count, heads, length),
            "grad_keys_values",
            info,
            [grad, queries, key_rows, value_rows, after, *landed],
            [big, big, big, big, big_states] + [state] * len(landed),
            [tokens16, tokens16],
            [big, big],
            scratch,
            8.0,
            LARGE,
        )
    return (grad_queries, grad_keys, grad_values, grad_gate)


def solution(mesh):
    return jax.shard_map(
        body,
        mesh=mesh,
        in_specs=(
            P(("seq", "head"), None),
            P("head", None),
            P("seq", "head"),
            P("seq", "head"),
            P("seq", "head"),
            P("seq", "head"),
            P(),
        ),
        out_specs=(P("seq", "head"), P("seq", "head"), P("seq", "head"), P("seq", "head")),
        check_vma=False,
    )
```

```python
import functools

import jax
import jax.numpy as jnp
from jax import lax
from jax.experimental import pallas as pl
from jax.experimental.pallas import tpu as pltpu
from jax.sharding import PartitionSpec as P

HEAD_DIM = 128
BLK = 512
LARGE = 1024
CHUNK = 256
EPS = 1e-06
F32 = jnp.float32
BF16 = jnp.bfloat16
VMEM_LIMIT = 16 * 1024 * 1024
PROJECT_VMEM = 16 * 1024 * 1024
PIECES = 2
COST_SCALE = 1.15e9


def dot(a, b):
    return lax.dot_general(a, b, (((1,), (0,)), ((), ())), preferred_element_type=F32)


def dot_nt(a, b):
    return lax.dot_general(a, b, (((1,), (1,)), ((), ())), preferred_element_type=F32)


def dot_tn(a, b):
    return lax.dot_general(a, b, (((0,), (0,)), ((), ())), preferred_element_type=F32)


def doc_of(info, count, pos):
    total = jnp.zeros_like(pos)
    for i in range(count):
        total = total + jnp.where(info[i] <= pos, 1, 0)
    return total


def same(a, b):
    return jnp.where(a == b, F32(1.0), F32(0.0))


def column_docs(info, count, start, size):
    return doc_of(info, count, start + lax.broadcasted_iota(jnp.int32, (size, 1), 0))


def row_docs(info, count, start, size):
    return doc_of(info, count, start + lax.broadcasted_iota(jnp.int32, (1, size), 1))


def causal_mask(info, count, start, transposed):
    down = lax.broadcasted_iota(jnp.int32, (CHUNK, CHUNK), 0)
    over = lax.broadcasted_iota(jnp.int32, (CHUNK, CHUNK), 1)
    equal = column_docs(info, count, start, CHUNK) == row_docs(info, count, start, CHUNK)
    return equal & ((down <= over) if transposed else (over <= down))


def chunk_rows(r):
    return slice(r * CHUNK, (r + 1) * CHUNK)


def lane_sums(x):
    return jnp.sum(x.T, axis=0, keepdims=True)


def to_columns(row):
    return jnp.broadcast_to(row, (HEAD_DIM, row.shape[1])).T


def head_slice(h):
    return slice(h * HEAD_DIM, (h + 1) * HEAD_DIM)


def key_state_kernel(count, heads, info, k_ref, v_ref, before_ref, total_ref, state):
    b = pl.program_id(0)

    @pl.when(b == 0)
    def _():
        state[...] = jnp.zeros_like(state)

    for r in range(BLK // CHUNK):
        rows = chunk_rows(r)
        start = info[count] + b * BLK + r * CHUNK
        last_doc = doc_of(info, count, start + CHUNK - 1)
        keep_out = same(column_docs(info, count, start, CHUNK), last_doc).astype(BF16)
        carry = same(doc_of(info, count, start - 1), last_doc)
        for h in range(heads):
            at = head_slice(h)
            before_ref[r, h] = state[h]
            state[h] = dot_tn(k_ref[rows, at] * keep_out, v_ref[rows, at]) + carry * state[h]
    total_ref[...] = state[...]


def attention_kernel(
    count, heads, info, q_ref, k_ref, v_ref, before_ref, into_ref, attn_ref, square_ref, low_ref
):
    first = info[count]
    size = q_ref.shape[0]
    for r in range(size // CHUNK):
        rows = chunk_rows(r)
        start = first + pl.program_id(0) * size + r * CHUNK
        prior = doc_of(info, count, start - 1)
        carry = same(prior, doc_of(info, count, first - 1))
        mask = causal_mask(info, count, start, False)
        keep_in = same(column_docs(info, count, start, CHUNK), prior)
        probs, carried = [], []
        for h in range(heads):
            at = head_slice(h)
            low = (before_ref[r, h] + carry * into_ref[h]).astype(BF16)
            low_ref[r, h] = low
            q = q_ref[rows, at]
            probs.append(jnp.where(mask, dot_nt(q, k_ref[rows, at]), 0.0).astype(BF16))
            carried.append(keep_in * dot(q, low))
        squares = jnp.zeros((CHUNK, HEAD_DIM), F32)
        for h in range(heads):
            at = head_slice(h)
            out = carried[h] + dot(probs[h], v_ref[rows, at])
            attn_ref[rows, at] = out
            squares = squares + out * out
        square_ref[:, rows] = lane_sums(squares)


def mix_heads(heads, info, near_ref, far_ref):
    core = info[info.shape[0] - 1]
    half = heads // 2
    for index, ref in enumerate((near_ref, far_ref)):
        for i in range(half):
            h = (core ^ index) * half + i
            at = pl.ds(pl.multiple_of(h * HEAD_DIM, HEAD_DIM), HEAD_DIM)
            yield ref.at[:, head_slice(i)], at


def cross_kernel(heads, info, near_ref, far_ref, gate_ref, attn_ref, square_ref, sums_ref):
    total = jnp.zeros((BLK, HEAD_DIM), F32)
    for mix, at in mix_heads(heads, info, near_ref, far_ref):
        total = total + mix[...].astype(F32) * gate_ref[:, at].astype(F32) * attn_ref[:, at]
    sums_ref[0:1, :] = square_ref[...]
    sums_ref[1:2, :] = lane_sums(total)


def grad_attn_kernel(
    count,
    heads,
    width,
    info,
    near_ref,
    far_ref,
    gate_ref,
    attn_ref,
    q_ref,
    sums_ref,
    grad_ref,
    gate_grad_ref,
    after_ref,
    total_ref,
    low_ref,
    state,
):
    @pl.when(pl.program_id(0) == 0)
    def _():
        state[...] = jnp.zeros_like(state)

    b = pl.num_programs(0) - 1 - pl.program_id(0)
    rms = jnp.sqrt(sums_ref[0:1, :] / width + EPS)
    inverse = to_columns(1.0 / rms)
    pull = to_columns(sums_ref[1:2, :] / (width * (rms * rms * rms)))
    for r in reversed(range(BLK // CHUNK)):
        rows = chunk_rows(r)
        start = info[count] + b * BLK + r * CHUNK
        prior = doc_of(info, count, start - 1)
        keep_in = same(column_docs(info, count, start, CHUNK), prior).astype(BF16)
        carry = same(doc_of(info, count, start + CHUNK - 1), prior)
        half = heads // 2
        for i, (mix, at) in enumerate(mix_heads(heads, info, near_ref, far_ref)):
            h = (info[count + 1] ^ (i // half)) * half + i % half
            scaled = mix[rows].astype(F32) * inverse[rows]
            attn = attn_ref[rows, at]
            gate_grad_ref[rows, at] = (scaled * attn).astype(BF16)
            grad = (scaled * gate_ref[rows, at].astype(F32) - attn * pull[rows]).astype(BF16)
            grad_ref[rows, at] = grad
            after_ref[r, h] = state[h]
            state[h] = dot_tn(q_ref[rows, at] * keep_in, grad) + carry * state[h]
    total_ref[...] = state[...]
    low_ref[...] = state[...].astype(BF16)


def grad_query_kernel(count, heads, info, grad_ref, k_ref, v_ref, low_ref, out_ref):
    size = grad_ref.shape[0]
    for r in range(size // CHUNK):
        rows = chunk_rows(r)
        start = info[count] + pl.program_id(0) * size + r * CHUNK
        prior = doc_of(info, count, start - 1)
        mask = causal_mask(info, count, start, False)
        keep_in = same(column_docs(info, count, start, CHUNK), prior)
        dprobs, carried = [], []
        for h in range(heads):
            at = head_slice(h)
            grad = grad_ref[rows, at]
            dprobs.append(jnp.where(mask, dot_nt(grad, v_ref[rows, at]), 0.0).astype(BF16))
            carried.append(keep_in * dot_nt(grad, low_ref[r, h]))
        for h in range(heads):
            at = head_slice(h)
            out_ref[rows, at] = (carried[h] + dot(dprobs[h], k_ref[rows, at])).astype(BF16)


def grad_key_value_kernel(
    count, heads, length, info, grad_ref, q_ref, k_ref, v_ref, after_ref, *refs
):
    *landed, dk_ref, dv_ref, into_ref = refs
    first = info[count]
    size = grad_ref.shape[0]

    @pl.when(pl.program_id(0) == 0)
    def _():
        place = lax.div(first, length)
        last_doc = doc_of(info, count, first + length - 1)
        total = None
        for index, ref in enumerate(landed):
            source = place ^ (index + 1)
            takes = jnp.where(source > place, F32(1.0), F32(0.0))
            takes = takes * same(doc_of(info, count, source * length - 1), last_doc)
            term = ref[...].astype(F32) * takes
            total = term if total is None else total + term
        into_ref[...] = total

    for r in range(size // CHUNK):
        rows = chunk_rows(r)
        start = first + pl.program_id(0) * size + r * CHUNK
        last_doc = doc_of(info, count, start + CHUNK - 1)
        carry = same(last_doc, doc_of(info, count, first + length - 1))
        mask = causal_mask(info, count, start, True)
        keep_out = same(column_docs(info, count, start, CHUNK), last_doc)
        for pair in range(0, heads, 2):
            parts = []
            for h in range(pair, min(pair + 2, heads)):
                at = head_slice(h)
                low = (after_ref[r, h] + carry * into_ref[h]).astype(BF16)
                k, v = k_ref[rows, at], v_ref[rows, at]
                dprob = jnp.where(mask, dot_nt(v, grad_ref[rows, at]), 0.0).astype(BF16)
                probs = jnp.where(mask, dot_nt(k, q_ref[rows, at]), 0.0).astype(BF16)
                parts.append(
                    (at, dprob, probs, keep_out * dot_nt(v, low), keep_out * dot(k, low))
                )
            for at, dprob, probs, from_v, from_k in parts:
                dk_ref[rows, at] = (from_v + dot(dprob, q_ref[rows, at])).astype(BF16)
                dv_ref[rows, at] = (from_k + dot(probs, grad_ref[rows, at])).astype(BF16)


def combine_kernel(count, length, size, info, total_ref, other_ref, into_ref, *outs):
    first = info[count]
    place = lax.div(first, length)
    group = lax.div(place, size)
    other_doc = doc_of(info, count, ((group ^ 1) + 1) * (size * length) - 1)
    my_doc = doc_of(info, count, (group + 1) * (size * length) - 1)
    later = same(group & 1, 1)
    reaches = later * same(other_doc, doc_of(info, count, first - 1))
    joined = same(other_doc, my_doc)
    total_share = later + (1.0 - later) * joined
    other_share = later * joined + (1.0 - later)
    other = other_ref[...].astype(F32)
    total = total_ref[...].astype(F32) * total_share + other * other_share
    outs[0][...] = total.astype(BF16)
    outs[1][...] = into_ref[...] + other * reaches


def combine(info, count, length, size, total, other, into):
    whole = pl.BlockSpec(total.shape, lambda i, s: (0, 0, 0))
    return pl.pallas_call(
        functools.partial(combine_kernel, count, length, size),
        grid_spec=pltpu.PrefetchScalarGridSpec(
            num_scalar_prefetch=1, grid=(1,), in_specs=[whole] * 3, out_specs=[whole] * 2
        ),
        out_shape=[
            jax.ShapeDtypeStruct(total.shape, BF16),
            jax.ShapeDtypeStruct(total.shape, F32),
        ],
        name="combine",
        cost_estimate=cost(1.0),
        compiler_params=pltpu.CompilerParams(vmem_limit_bytes=VMEM_LIMIT),
    )(info, total, other, into)


def gather_kernel(info, *refs):
    sets, out, arrived = refs[:4], refs[4], refs[5]
    rows = sets[0].shape[0]
    copies = []
    for index, ref in enumerate(sets):
        place = 2 * (info[2] ^ (index // 2)) + (info[0] ^ (index % 2))
        at = pl.ds(pl.multiple_of(place * rows, rows), rows)
        copies.append(pltpu.make_async_copy(ref, out.at[at, :], arrived.at[index]))
    for copy in copies:
        copy.start()
    for copy in copies:
        copy.wait()


def gather_rows(info, sets):
    rows, depth = sets[0].shape
    return pl.pallas_call(
        gather_kernel,
        grid_spec=pltpu.PrefetchScalarGridSpec(
            num_scalar_prefetch=1,
            grid=(1,),
            in_specs=[pl.BlockSpec(memory_space=pl.ANY)] * 4,
            out_specs=pl.BlockSpec(memory_space=pltpu.VMEM),
            scratch_shapes=[pltpu.SemaphoreType.DMA((4,))],
        ),
        out_shape=jax.ShapeDtypeStruct((4 * rows, depth), BF16),
        name="gather_rows",
        cost_estimate=cost(3.0),
        compiler_params=pltpu.CompilerParams(vmem_limit_bytes=PROJECT_VMEM),
    )(info, *sets)


def project_kernel(split, info, rows_ref, *refs):
    count = len(refs) // (split + 1)
    shards, outs = refs[: count * split], refs[count * split :]
    part = rows_ref.shape[1] // split
    total = None
    for j in range(split):
        if split == 1:
            left = rows_ref[...]
        else:
            left = rows_ref[:, pl.ds(pl.multiple_of((info[1] ^ j) * part, part), part)]
        weights = [shards[i * split + j][...] for i in range(count)]
        weights = weights[0] if count == 1 else jnp.concatenate(weights, axis=0)
        term = dot_nt(left, weights)
        total = term if total is None else total + term
    width = total.shape[1] // count
    for i, out in enumerate(outs):
        out[...] = total[:, i * width : (i + 1) * width].astype(BF16)


def project(info, rows, shards):
    args = [rows, *(part for parts in shards for part in parts)]
    outs = [jax.ShapeDtypeStruct((rows.shape[0], shards[0][0].shape[0]), BF16)] * len(shards)
    return pl.pallas_call(
        functools.partial(project_kernel, len(shards[0])),
        grid_spec=pltpu.PrefetchScalarGridSpec(
            num_scalar_prefetch=1,
            grid=(1,),
            in_specs=[pl.BlockSpec(memory_space=pltpu.VMEM)]
            * len(args),
            out_specs=[pl.BlockSpec(memory_space=pltpu.VMEM) for o in outs],
        ),
        out_shape=outs,
        name="project",
        cost_estimate=cost(3.0),
        compiler_params=pltpu.CompilerParams(vmem_limit_bytes=PROJECT_VMEM),
    )(info, *args)


def add_kernel(*refs):
    total = refs[0][...]
    for ref in refs[1:-1]:
        total = total + ref[...]
    refs[-1][...] = total


def add_all(arrays):
    return pl.pallas_call(
        add_kernel,
        in_specs=[pl.BlockSpec(memory_space=pltpu.VMEM)] * len(arrays),
        out_specs=pl.BlockSpec(memory_space=pltpu.VMEM),
        out_shape=jax.ShapeDtypeStruct(arrays[0].shape, arrays[0].dtype),
        name="add_all",
        cost_estimate=cost(0.7),
        compiler_params=pltpu.CompilerParams(vmem_limit_bytes=2 * 1024 * 1024),
    )(*arrays)


def cost(micros):
    return pl.CostEstimate(
        flops=int(micros * COST_SCALE), bytes_accessed=0, transcendentals=0
    )


def grad_mixture(out_grad, out_weight, length, early, middle, late):
    n_head = lax.axis_size("head")
    n_pairs = n_head // 2
    rows, depth = out_grad.shape
    width = out_weight.shape[0]
    half = width // 2
    piece_size = half // PIECES
    part_depth = depth // 2
    me = lax.axis_index("head")
    side, pair = me % 2, me // 2
    core = lax.axis_index("seq") % 2
    slot = (lax.axis_index("seq") // 2) % 2
    info = jnp.stack([side, slot, core]).astype(jnp.int32)
    pair, core, slot = (value.astype(jnp.uint32) for value in (pair, core, slot))
    nothing = jnp.uint32(0)
    hops = sorted(range(1, n_pairs), key=lambda k: (bin(k).count("1"), -k))
    order = [(0, hop) for hop in hops if hop & (hop - 1) == 0]
    order += [(1, hop) for hop in hops[:1]]
    order += [(0, hop) for hop in hops if hop & (hop - 1) != 0]
    order += [(1, hop) for hop in hops[1:]]
    order[0], order[1] = order[1], order[0]
    order[-2], order[-1] = order[-1], order[-2]
    waves = [order[i : i + 2] for i in range(0, len(order), 2)]

    fetched = {
        (piece, 0): lax.dynamic_slice(
            out_weight,
            (core * half + jnp.uint32(piece * piece_size), slot * part_depth),
            (piece_size, part_depth),
        )
        for piece in range(PIECES)
    }
    rows_after, _ = lax.optimization_barrier((out_grad, fetched[0, 0]))
    sets = [out_grad, flip(rows_after, "head", 1), None, None]
    across = {}
    arrived = {}
    for step in range(len(waves) + 2):
        wave = waves[step] if step < len(waves) else []
        landed = waves[step - 1] if 0 < step <= len(waves) else []
        spread = waves[step - 2] if 1 < step else []
        for piece, hop in wave:
            low = hop & -hop
            fetched[piece, hop] = flip(fetched[piece, hop ^ low], "head", 2 * low)
        for key in landed:
            across[key] = flip(fetched[key], "seq", 2)
        made = []
        if step == 0:
            sets[2] = flip(rows_after, "seq", 1)
            made.append(sets[2])
        if step == 1:
            weight, _ = lax.optimization_barrier((out_weight, fetched[waves[0][0]]))
            mine = lax.dynamic_slice(weight, (core * half, nothing), (half, depth))
            made += [mine, sets[1], early(fetched[waves[0][0]])]
        if step == 2:
            sets[3] = flip(sets[1], "seq", 1)
            all_rows = gather_rows(info, sets)
        last_step = step == len(waves) + 1
        if spread:
            shards = [[fetched[key], across[key]] for key in spread]
            products = project(info, all_rows, shards)
            made += products
            for key, product in zip(spread, products):
                arrived[key] = flip(product, "head", 2 * key[1])
        if step >= 2 and size < lax.axis_size("seq") and (step >= 4 or size == 1):
            total, into = middle(total, flip(total, "seq", size), into, size)
            size *= 2
        if last_step:
            while size < lax.axis_size("seq"):
                total, into = middle(total, flip(total, "seq", size), into, size)
                size *= 2
            attended = late(products[0], into)
        if step == 3:
            arrived[0, 0] = project(info, all_rows, [[mine]])[0]
            made.append(arrived[0, 0])
        if step < len(waves) + 1:
            names = [key for key in fetched if key not in wave]
            carried = (total, into) if step > 1 else ()
            keep, new, far, made, carried = lax.optimization_barrier(
                (
                    [fetched[key] for key in names],
                    [fetched[key] for key in wave] if step > 0 else [],
                    [across[key] for key in landed],
                    made,
                    carried,
                )
            )
            if step == 0:
                sets[2] = made[0]
            if step == 1:
                mine, sets[1], total = made
                into, size = jnp.zeros_like(total), 1
            elif step > 1:
                total, into = carried
            fetched.update(zip(names, keep))
            if step > 0:
                fetched.update(zip(wave, new))
            across.update(zip(landed, far))
    last = [arrived[key] for key in spread]
    last, _ = lax.optimization_barrier((last, attended))
    arrived.update(zip(spread, last))
    mixes = []
    for source in (None, 1):
        mix = jnp.zeros((length, half), BF16)
        for (piece, hop), product in arrived.items():
            which = core if source is None else jnp.uint32(1) - core
            product = lax.dynamic_slice(
                product, (which * (2 * rows), nothing), (2 * rows, product.shape[1])
            )
            mix = lax.dynamic_update_slice(
                mix, product, ((pair ^ jnp.uint32(hop)) * (2 * rows), jnp.uint32(piece * piece_size))
            )
        mixes.append(mix)
    return mixes[0], flip(mixes[1], "seq", 1)


def call(kernel, name, info, args, in_specs, outs, out_specs, scratch=(), micros=3.0, size=BLK):
    nblocks = max(a.shape[0] for a in args if a.ndim == 2) // size
    return pl.pallas_call(
        kernel,
        grid_spec=pltpu.PrefetchScalarGridSpec(
            num_scalar_prefetch=1,
            grid=(nblocks,),
            in_specs=in_specs,
            out_specs=out_specs,
            scratch_shapes=list(scratch),
        ),
        out_shape=outs,
        name=name,
        cost_estimate=cost(micros),
        compiler_params=pltpu.CompilerParams(vmem_limit_bytes=VMEM_LIMIT),
    )(info, *args)


def shaped(shape, dtype):
    return jax.ShapeDtypeStruct(shape, dtype)


def flip(a, axis, bit):
    return lax.ppermute(a, axis, [(i, i ^ bit) for i in range(lax.axis_size(axis))])


def subsets(items):
    found = [[]]
    for item in items:
        found += [[*one, item] for one in found]
    return found[1:]


def head_sum(sums):
    bits = [1 << i for i in range(lax.axis_size("head").bit_length() - 1)]
    for group in (bits[1:3], bits[:1], bits[3:]):
        spans = [sum(chosen) for chosen in subsets(group)]
        if spans:
            sums = add_all([sums, *(flip(sums, "head", span) for span in spans)])
    return sums


def body(out_grad, out_weight, queries, key_rows, value_rows, gate_out, doc_starts):
    length, width = queries.shape
    heads = width // HEAD_DIM
    nblocks = length // BLK
    count = doc_starts.shape[0]
    full_width = width * lax.axis_size("head")
    place = lax.axis_index("seq")
    first = place * length
    info = jnp.concatenate([doc_starts, jnp.stack([first, place % 2]).astype(jnp.int32)])

    block = pl.BlockSpec((BLK, width), lambda b, s: (b, 0))
    half_block = pl.BlockSpec((BLK, width // 2), lambda b, s: (b, 0))
    line = pl.BlockSpec((1, BLK), lambda b, s: (0, b))
    states = pl.BlockSpec((BLK // CHUNK, heads, HEAD_DIM, HEAD_DIM), lambda b, s: (b, 0, 0, 0))
    state = pl.BlockSpec((heads, HEAD_DIM, HEAD_DIM), lambda b, s: (0, 0, 0))
    one_state = shaped((heads, HEAD_DIM, HEAD_DIM), F32)
    low_state = shaped((heads, HEAD_DIM, HEAD_DIM), BF16)
    all_states = shaped((length // CHUNK, heads, HEAD_DIM, HEAD_DIM), F32)
    low_states = shaped((length // CHUNK, heads, HEAD_DIM, HEAD_DIM), BF16)
    tokens16 = shaped((length, width), BF16)
    tokens32 = shaped((length, width), F32)
    row = shaped((1, length), F32)
    scratch = [pltpu.VMEM((heads, HEAD_DIM, HEAD_DIM), F32)]

    kept = {}

    def early(landed):
        keys, values, _ = lax.optimization_barrier((key_rows, value_rows, landed))
        with jax.named_scope("key_states"):
            before, key_total = call(
                functools.partial(key_state_kernel, count, heads),
                "key_states",
                info,
                [keys, values],
                [block, block],
                [all_states, one_state],
                [states, state],
                scratch,
                12.0,
            )
        kept["before"] = before
        return key_total

    def middle(total, other, into, size):
        return combine(info, count, length, size, total, other, into)

    def late(product, into):
        kept["into"] = into
        tokens, _ = lax.optimization_barrier((queries, product))
        with jax.named_scope("attention"):
            kept["attn"], kept["square"], kept["low"] = call(
                functools.partial(attention_kernel, count, heads),
                "attention",
                info,
                [tokens, key_rows, value_rows, kept["before"], kept["into"]],
                [block, block, block, states, state],
                [tokens32, row, low_states],
                [block, line, states],
                (),
                8.0,
            )
        return kept["square"]

    near, far = grad_mixture(out_grad, out_weight, length, early, middle, late)
    attn, square, low = kept["attn"], kept["square"], kept["low"]

    with jax.named_scope("cross"):
        sums = call(
            functools.partial(cross_kernel, heads),
            "cross",
            info,
            [near, far, gate_out, attn, square],
            [half_block, half_block, block, block, line],
            [shaped((2, length), F32)],
            [pl.BlockSpec((2, BLK), lambda b, s: (0, b))],
        )[0]

    sums = head_sum(sums)

    back = lambda spec_shape, f: pl.BlockSpec(spec_shape, lambda b, s: f(nblocks - 1 - b))
    block_r = back((BLK, width), lambda b: (b, 0))
    half_r = back((BLK, width // 2), lambda b: (b, 0))
    line_r = back((2, BLK), lambda b: (0, b))
    states_r = back((BLK // CHUNK, heads, HEAD_DIM, HEAD_DIM), lambda b: (b, 0, 0, 0))
    with jax.named_scope("grad_attn"):
        grad, grad_gate, after, query_total, query_low = call(
            functools.partial(grad_attn_kernel, count, heads, full_width),
            "grad_attn",
            info,
            [near, far, gate_out, attn, queries, sums],
            [half_r, half_r, block_r, block_r, block_r, line_r],
            [tokens16, tokens16, all_states, one_state, low_state],
            [block_r, block_r, states_r, state, state],
            scratch,
            4.0,
        )
    landed = [
        flip(query_total if step == 1 else query_low, "seq", step)
        for step in range(1, lax.axis_size("seq"))
    ]
    big = pl.BlockSpec((LARGE, width), lambda b, s: (b, 0))
    big_states = pl.BlockSpec(
        (LARGE // CHUNK, heads, HEAD_DIM, HEAD_DIM), lambda b, s: (b, 0, 0, 0)
    )
    with jax.named_scope("grad_queries"):
        grad_queries = call(
            functools.partial(grad_query_kernel, count, heads),
            "grad_queries",
            info,
            [grad, key_rows, value_rows, low],
            [big, big, big, big_states],
            [tokens16],
            [big],
            (),
            8.0,
            LARGE,
        )[0]
    with jax.named_scope("grad_keys_values"):
        grad_keys, grad_values = call(
            functools.partial(grad_key_value_kernel, count, heads, length),
            "grad_keys_values",
            info,
            [grad, queries, key_rows, value_rows, after, *landed],
            [big, big, big, big, big_states] + [state] * len(landed),
            [tokens16, tokens16],
            [big, big],
            scratch,
            8.0,
            LARGE,
        )
    return (grad_queries, grad_keys, grad_values, grad_gate)


def solution(mesh):
    return jax.shard_map(
        body,
        mesh=mesh,
        in_specs=(
            P(("seq", "head"), None),
            P("head", None),
            P("seq", "head"),
            P("seq", "head"),
            P("seq", "head"),
            P("seq", "head"),
            P(),
        ),
        out_specs=(P("seq", "head"), P("seq", "head"), P("seq", "head"), P("seq", "head")),
        check_vma=False,
    )
```

```python
import functools

import jax
import jax.numpy as jnp
from jax import lax
from jax.experimental import pallas as pl
from jax.experimental.pallas import tpu as pltpu
from jax.sharding import PartitionSpec as P

HEAD_DIM = 128
BLK = 512
LARGE = 1024
CHUNK = 256
EPS = 1e-06
F32 = jnp.float32
BF16 = jnp.bfloat16
VMEM_LIMIT = 16 * 1024 * 1024
PROJECT_VMEM = 16 * 1024 * 1024
PIECES = 2
COST_SCALE = 1.15e9


def dot(a, b):
    return lax.dot_general(a, b, (((1,), (0,)), ((), ())), preferred_element_type=F32)


def dot_nt(a, b):
    return lax.dot_general(a, b, (((1,), (1,)), ((), ())), preferred_element_type=F32)


def dot_tn(a, b):
    return lax.dot_general(a, b, (((0,), (0,)), ((), ())), preferred_element_type=F32)


def doc_of(info, count, pos):
    total = jnp.zeros_like(pos)
    for i in range(count):
        total = total + jnp.where(info[i] <= pos, 1, 0)
    return total


def same(a, b):
    return jnp.where(a == b, F32(1.0), F32(0.0))


def column_docs(info, count, start, size):
    return doc_of(info, count, start + lax.broadcasted_iota(jnp.int32, (size, 1), 0))


def row_docs(info, count, start, size):
    return doc_of(info, count, start + lax.broadcasted_iota(jnp.int32, (1, size), 1))


def causal_mask(info, count, start, transposed):
    down = lax.broadcasted_iota(jnp.int32, (CHUNK, CHUNK), 0)
    over = lax.broadcasted_iota(jnp.int32, (CHUNK, CHUNK), 1)
    equal = column_docs(info, count, start, CHUNK) == row_docs(info, count, start, CHUNK)
    return equal & ((down <= over) if transposed else (over <= down))


def chunk_rows(r):
    return slice(r * CHUNK, (r + 1) * CHUNK)


def lane_sums(x):
    return jnp.sum(x.T, axis=0, keepdims=True)


def to_columns(row):
    return jnp.broadcast_to(row, (HEAD_DIM, row.shape[1])).T


def head_slice(h):
    return slice(h * HEAD_DIM, (h + 1) * HEAD_DIM)


def key_state_kernel(count, heads, info, k_ref, v_ref, before_ref, total_ref, state):
    b = pl.program_id(0)

    @pl.when(b == 0)
    def _():
        state[...] = jnp.zeros_like(state)

    for r in range(BLK // CHUNK):
        rows = chunk_rows(r)
        start = info[count] + b * BLK + r * CHUNK
        last_doc = doc_of(info, count, start + CHUNK - 1)
        keep_out = same(column_docs(info, count, start, CHUNK), last_doc).astype(BF16)
        carry = same(doc_of(info, count, start - 1), last_doc)
        for h in range(heads):
            at = head_slice(h)
            before_ref[r, h] = state[h]
            state[h] = dot_tn(k_ref[rows, at] * keep_out, v_ref[rows, at]) + carry * state[h]
    total_ref[...] = state[...]


def attention_kernel(
    count, heads, info, q_ref, k_ref, v_ref, before_ref, into_ref, attn_ref, square_ref, low_ref
):
    first = info[count]
    size = q_ref.shape[0]
    for r in range(size // CHUNK):
        rows = chunk_rows(r)
        start = first + pl.program_id(0) * size + r * CHUNK
        prior = doc_of(info, count, start - 1)
        carry = same(prior, doc_of(info, count, first - 1))
        mask = causal_mask(info, count, start, False)
        keep_in = same(column_docs(info, count, start, CHUNK), prior)
        probs, carried = [], []
        for h in range(heads):
            at = head_slice(h)
            low = (before_ref[r, h] + carry * into_ref[h]).astype(BF16)
            low_ref[r, h] = low
            q = q_ref[rows, at]
            probs.append(jnp.where(mask, dot_nt(q, k_ref[rows, at]), 0.0).astype(BF16))
            carried.append(keep_in * dot(q, low))
        squares = jnp.zeros((CHUNK, HEAD_DIM), F32)
        for h in range(heads):
            at = head_slice(h)
            out = carried[h] + dot(probs[h], v_ref[rows, at])
            attn_ref[rows, at] = out
            squares = squares + out * out
        square_ref[:, rows] = lane_sums(squares)


def mix_heads(heads, info, near_ref, far_ref):
    core = info[info.shape[0] - 1]
    half = heads // 2
    for index, ref in enumerate((near_ref, far_ref)):
        for i in range(half):
            h = (core ^ index) * half + i
            at = pl.ds(pl.multiple_of(h * HEAD_DIM, HEAD_DIM), HEAD_DIM)
            yield ref.at[:, head_slice(i)], at


def cross_kernel(heads, info, near_ref, far_ref, gate_ref, attn_ref, square_ref, sums_ref):
    total = jnp.zeros((BLK, HEAD_DIM), F32)
    for mix, at in mix_heads(heads, info, near_ref, far_ref):
        total = total + mix[...].astype(F32) * gate_ref[:, at].astype(F32) * attn_ref[:, at]
    sums_ref[0:1, :] = square_ref[...]
    sums_ref[1:2, :] = lane_sums(total)


def grad_attn_kernel(
    count,
    heads,
    width,
    info,
    near_ref,
    far_ref,
    gate_ref,
    attn_ref,
    q_ref,
    sums_ref,
    grad_ref,
    gate_grad_ref,
    after_ref,
    total_ref,
    low_ref,
    state,
):
    @pl.when(pl.program_id(0) == 0)
    def _():
        state[...] = jnp.zeros_like(state)

    b = pl.num_programs(0) - 1 - pl.program_id(0)
    rms = jnp.sqrt(sums_ref[0:1, :] / width + EPS)
    inverse = to_columns(1.0 / rms)
    pull = to_columns(sums_ref[1:2, :] / (width * (rms * rms * rms)))
    for r in reversed(range(BLK // CHUNK)):
        rows = chunk_rows(r)
        start = info[count] + b * BLK + r * CHUNK
        prior = doc_of(info, count, start - 1)
        keep_in = same(column_docs(info, count, start, CHUNK), prior).astype(BF16)
        carry = same(doc_of(info, count, start + CHUNK - 1), prior)
        half = heads // 2
        for i, (mix, at) in enumerate(mix_heads(heads, info, near_ref, far_ref)):
            h = (info[count + 1] ^ (i // half)) * half + i % half
            scaled = mix[rows].astype(F32) * inverse[rows]
            attn = attn_ref[rows, at]
            gate_grad_ref[rows, at] = (scaled * attn).astype(BF16)
            grad = (scaled * gate_ref[rows, at].astype(F32) - attn * pull[rows]).astype(BF16)
            grad_ref[rows, at] = grad
            after_ref[r, h] = state[h]
            state[h] = dot_tn(q_ref[rows, at] * keep_in, grad) + carry * state[h]
    total_ref[...] = state[...]
    low_ref[...] = state[...].astype(BF16)


def grad_query_kernel(count, heads, info, grad_ref, k_ref, v_ref, low_ref, out_ref):
    size = grad_ref.shape[0]
    for r in range(size // CHUNK):
        rows = chunk_rows(r)
        start = info[count] + pl.program_id(0) * size + r * CHUNK
        prior = doc_of(info, count, start - 1)
        mask = causal_mask(info, count, start, False)
        keep_in = same(column_docs(info, count, start, CHUNK), prior)
        dprobs, carried = [], []
        for h in range(heads):
            at = head_slice(h)
            grad = grad_ref[rows, at]
            dprobs.append(jnp.where(mask, dot_nt(grad, v_ref[rows, at]), 0.0).astype(BF16))
            carried.append(keep_in * dot_nt(grad, low_ref[r, h]))
        for h in range(heads):
            at = head_slice(h)
            out_ref[rows, at] = (carried[h] + dot(dprobs[h], k_ref[rows, at])).astype(BF16)


def grad_key_value_kernel(
    count, heads, length, info, grad_ref, q_ref, k_ref, v_ref, after_ref, *refs
):
    *landed, dk_ref, dv_ref, into_ref = refs
    first = info[count]
    size = grad_ref.shape[0]

    @pl.when(pl.program_id(0) == 0)
    def _():
        place = lax.div(first, length)
        last_doc = doc_of(info, count, first + length - 1)
        total = None
        for index, ref in enumerate(landed):
            source = place ^ (index + 1)
            takes = jnp.where(source > place, F32(1.0), F32(0.0))
            takes = takes * same(doc_of(info, count, source * length - 1), last_doc)
            term = ref[...].astype(F32) * takes
            total = term if total is None else total + term
        into_ref[...] = total

    for r in range(size // CHUNK):
        rows = chunk_rows(r)
        start = first + pl.program_id(0) * size + r * CHUNK
        last_doc = doc_of(info, count, start + CHUNK - 1)
        carry = same(last_doc, doc_of(info, count, first + length - 1))
        mask = causal_mask(info, count, start, True)
        keep_out = same(column_docs(info, count, start, CHUNK), last_doc)
        for pair in range(0, heads, 2):
            parts = []
            for h in range(pair, min(pair + 2, heads)):
                at = head_slice(h)
                low = (after_ref[r, h] + carry * into_ref[h]).astype(BF16)
                k, v = k_ref[rows, at], v_ref[rows, at]
                dprob = jnp.where(mask, dot_nt(v, grad_ref[rows, at]), 0.0).astype(BF16)
                probs = jnp.where(mask, dot_nt(k, q_ref[rows, at]), 0.0).astype(BF16)
                parts.append(
                    (at, dprob, probs, keep_out * dot_nt(v, low), keep_out * dot(k, low))
                )
            for at, dprob, probs, from_v, from_k in parts:
                dk_ref[rows, at] = (from_v + dot(dprob, q_ref[rows, at])).astype(BF16)
                dv_ref[rows, at] = (from_k + dot(probs, grad_ref[rows, at])).astype(BF16)


def combine_kernel(count, length, size, info, total_ref, other_ref, into_ref, *outs):
    first = info[count]
    place = lax.div(first, length)
    group = lax.div(place, size)
    other_doc = doc_of(info, count, ((group ^ 1) + 1) * (size * length) - 1)
    my_doc = doc_of(info, count, (group + 1) * (size * length) - 1)
    later = same(group & 1, 1)
    reaches = later * same(other_doc, doc_of(info, count, first - 1))
    joined = same(other_doc, my_doc)
    total_share = later + (1.0 - later) * joined
    other_share = later * joined + (1.0 - later)
    other = other_ref[...].astype(F32)
    total = total_ref[...].astype(F32) * total_share + other * other_share
    outs[0][...] = total.astype(BF16)
    outs[1][...] = into_ref[...] + other * reaches


def combine(info, count, length, size, total, other, into):
    whole = pl.BlockSpec(total.shape, lambda i, s: (0, 0, 0))
    return pl.pallas_call(
        functools.partial(combine_kernel, count, length, size),
        grid_spec=pltpu.PrefetchScalarGridSpec(
            num_scalar_prefetch=1, grid=(1,), in_specs=[whole] * 3, out_specs=[whole] * 2
        ),
        out_shape=[
            jax.ShapeDtypeStruct(total.shape, BF16),
            jax.ShapeDtypeStruct(total.shape, F32),
        ],
        name="combine",
        cost_estimate=cost(1.0),
        compiler_params=pltpu.CompilerParams(vmem_limit_bytes=VMEM_LIMIT),
    )(info, total, other, into)


def gather_kernel(info, *refs):
    sets, out, arrived = refs[:4], refs[4], refs[5]
    rows = sets[0].shape[0]
    copies = []
    for index, ref in enumerate(sets):
        place = 2 * (info[2] ^ (index // 2)) + (info[0] ^ (index % 2))
        at = pl.ds(pl.multiple_of(place * rows, rows), rows)
        copies.append(pltpu.make_async_copy(ref, out.at[at, :], arrived.at[index]))
    for copy in copies:
        copy.start()
    for copy in copies:
        copy.wait()


def gather_rows(info, sets):
    rows, depth = sets[0].shape
    return pl.pallas_call(
        gather_kernel,
        grid_spec=pltpu.PrefetchScalarGridSpec(
            num_scalar_prefetch=1,
            grid=(1,),
            in_specs=[pl.BlockSpec(memory_space=pl.ANY)] * 4,
            out_specs=pl.BlockSpec(memory_space=pltpu.VMEM),
            scratch_shapes=[pltpu.SemaphoreType.DMA((4,))],
        ),
        out_shape=jax.ShapeDtypeStruct((4 * rows, depth), BF16),
        name="gather_rows",
        cost_estimate=cost(3.0),
        compiler_params=pltpu.CompilerParams(vmem_limit_bytes=PROJECT_VMEM),
    )(info, *sets)


def project_kernel(split, info, rows_ref, *refs):
    count = len(refs) // (split + 1)
    shards, outs = refs[: count * split], refs[count * split :]
    part = rows_ref.shape[1] // split
    total = None
    for j in range(split):
        if split == 1:
            left = rows_ref[...]
        else:
            left = rows_ref[:, pl.ds(pl.multiple_of((info[1] ^ j) * part, part), part)]
        weights = [shards[i * split + j][...] for i in range(count)]
        weights = weights[0] if count == 1 else jnp.concatenate(weights, axis=0)
        term = dot_nt(left, weights)
        total = term if total is None else total + term
    width = total.shape[1] // count
    for i, out in enumerate(outs):
        out[...] = total[:, i * width : (i + 1) * width].astype(BF16)


def project(info, rows, shards):
    args = [rows, *(part for parts in shards for part in parts)]
    outs = [jax.ShapeDtypeStruct((rows.shape[0], shards[0][0].shape[0]), BF16)] * len(shards)
    return pl.pallas_call(
        functools.partial(project_kernel, len(shards[0])),
        grid_spec=pltpu.PrefetchScalarGridSpec(
            num_scalar_prefetch=1,
            grid=(1,),
            in_specs=[pl.BlockSpec(memory_space=pltpu.VMEM)]
            * len(args),
            out_specs=[pl.BlockSpec(memory_space=pltpu.VMEM) for o in outs],
        ),
        out_shape=outs,
        name="project",
        cost_estimate=cost(5.0),
        compiler_params=pltpu.CompilerParams(vmem_limit_bytes=PROJECT_VMEM),
    )(info, *args)


def add_kernel(*refs):
    total = refs[0][...]
    for ref in refs[1:-1]:
        total = total + ref[...]
    refs[-1][...] = total


def add_all(arrays):
    return pl.pallas_call(
        add_kernel,
        in_specs=[pl.BlockSpec(memory_space=pltpu.VMEM)] * len(arrays),
        out_specs=pl.BlockSpec(memory_space=pltpu.VMEM),
        out_shape=jax.ShapeDtypeStruct(arrays[0].shape, arrays[0].dtype),
        name="add_all",
        cost_estimate=cost(0.7),
        compiler_params=pltpu.CompilerParams(vmem_limit_bytes=2 * 1024 * 1024),
    )(*arrays)


def cost(micros):
    return pl.CostEstimate(
        flops=int(micros * COST_SCALE), bytes_accessed=0, transcendentals=0
    )


def grad_mixture(out_grad, out_weight, length, early, middle, late):
    n_head = lax.axis_size("head")
    n_pairs = n_head // 2
    rows, depth = out_grad.shape
    width = out_weight.shape[0]
    half = width // 2
    piece_size = half // PIECES
    part_depth = depth // 2
    me = lax.axis_index("head")
    side, pair = me % 2, me // 2
    core = lax.axis_index("seq") % 2
    slot = (lax.axis_index("seq") // 2) % 2
    info = jnp.stack([side, slot, core]).astype(jnp.int32)
    pair, core, slot = (value.astype(jnp.uint32) for value in (pair, core, slot))
    nothing = jnp.uint32(0)
    hops = sorted(range(1, n_pairs), key=lambda k: (bin(k).count("1"), -k))
    order = [(0, hop) for hop in hops if hop & (hop - 1) == 0]
    order += [(1, hop) for hop in hops[:1]]
    order += [(0, hop) for hop in hops if hop & (hop - 1) != 0]
    order += [(1, hop) for hop in hops[1:]]
    order[0], order[1] = order[1], order[0]
    order[-2], order[-1] = order[-1], order[-2]
    waves = [order[i : i + 2] for i in range(0, len(order), 2)]

    fetched = {
        (piece, 0): lax.dynamic_slice(
            out_weight,
            (core * half + jnp.uint32(piece * piece_size), slot * part_depth),
            (piece_size, part_depth),
        )
        for piece in range(PIECES)
    }
    rows_after, _ = lax.optimization_barrier((out_grad, fetched[0, 0]))
    sets = [out_grad, flip(rows_after, "head", 1), None, None]
    across = {}
    arrived = {}
    for step in range(len(waves) + 2):
        wave = waves[step] if step < len(waves) else []
        landed = waves[step - 1] if 0 < step <= len(waves) else []
        spread = waves[step - 2] if 1 < step else []
        for piece, hop in wave:
            low = hop & -hop
            fetched[piece, hop] = flip(fetched[piece, hop ^ low], "head", 2 * low)
        for key in landed:
            across[key] = flip(fetched[key], "seq", 2)
        made = []
        if step == 0:
            sets[2] = flip(rows_after, "seq", 1)
            made.append(sets[2])
        if step == 1:
            weight, _ = lax.optimization_barrier((out_weight, fetched[waves[0][0]]))
            mine = lax.dynamic_slice(weight, (core * half, nothing), (half, depth))
            made += [mine, sets[1], early(fetched[waves[0][0]])]
        if step == 2:
            sets[3] = flip(sets[1], "seq", 1)
            all_rows = gather_rows(info, sets)
        last_step = step == len(waves) + 1
        if spread:
            shards = [[fetched[key], across[key]] for key in spread]
            products = project(info, all_rows, shards)
            made += products
            for key, product in zip(spread, products):
                arrived[key] = flip(product, "head", 2 * key[1])
        if step >= 2 and size < lax.axis_size("seq") and (step >= 4 or size == 1):
            total, into = middle(total, flip(total, "seq", size), into, size)
            size *= 2
        if last_step:
            while size < lax.axis_size("seq"):
                total, into = middle(total, flip(total, "seq", size), into, size)
                size *= 2
            attended = late(products[0], into)
        if step == 3:
            arrived[0, 0] = project(info, all_rows, [[mine]])[0]
            made.append(arrived[0, 0])
        if step < len(waves) + 1:
            names = [key for key in fetched if key not in wave]
            carried = (total, into) if step > 1 else ()
            keep, new, far, made, carried = lax.optimization_barrier(
                (
                    [fetched[key] for key in names],
                    [fetched[key] for key in wave] if step > 0 else [],
                    [across[key] for key in landed],
                    made,
                    carried,
                )
            )
            if step == 0:
                sets[2] = made[0]
            if step == 1:
                mine, sets[1], total = made
                into, size = jnp.zeros_like(total), 1
            elif step > 1:
                total, into = carried
            fetched.update(zip(names, keep))
            if step > 0:
                fetched.update(zip(wave, new))
            across.update(zip(landed, far))
    last = [arrived[key] for key in spread]
    last, _ = lax.optimization_barrier((last, attended))
    arrived.update(zip(spread, last))
    mixes = []
    for source in (None, 1):
        mix = jnp.zeros((length, half), BF16)
        for (piece, hop), product in arrived.items():
            which = core if source is None else jnp.uint32(1) - core
            product = lax.dynamic_slice(
                product, (which * (2 * rows), nothing), (2 * rows, product.shape[1])
            )
            mix = lax.dynamic_update_slice(
                mix, product, ((pair ^ jnp.uint32(hop)) * (2 * rows), jnp.uint32(piece * piece_size))
            )
        mixes.append(mix)
    return mixes[0], flip(mixes[1], "seq", 1)


def call(kernel, name, info, args, in_specs, outs, out_specs, scratch=(), micros=3.0, size=BLK):
    nblocks = max(a.shape[0] for a in args if a.ndim == 2) // size
    return pl.pallas_call(
        kernel,
        grid_spec=pltpu.PrefetchScalarGridSpec(
            num_scalar_prefetch=1,
            grid=(nblocks,),
            in_specs=in_specs,
            out_specs=out_specs,
            scratch_shapes=list(scratch),
        ),
        out_shape=outs,
        name=name,
        cost_estimate=cost(micros),
        compiler_params=pltpu.CompilerParams(vmem_limit_bytes=VMEM_LIMIT),
    )(info, *args)


def shaped(shape, dtype):
    return jax.ShapeDtypeStruct(shape, dtype)


def flip(a, axis, bit):
    return lax.ppermute(a, axis, [(i, i ^ bit) for i in range(lax.axis_size(axis))])


def subsets(items):
    found = [[]]
    for item in items:
        found += [[*one, item] for one in found]
    return found[1:]


def head_sum(sums):
    bits = [1 << i for i in range(lax.axis_size("head").bit_length() - 1)]
    for group in (bits[1:3], bits[:1], bits[3:]):
        spans = [sum(chosen) for chosen in subsets(group)]
        if spans:
            sums = add_all([sums, *(flip(sums, "head", span) for span in spans)])
    return sums


def body(out_grad, out_weight, queries, key_rows, value_rows, gate_out, doc_starts):
    length, width = queries.shape
    heads = width // HEAD_DIM
    nblocks = length // BLK
    count = doc_starts.shape[0]
    full_width = width * lax.axis_size("head")
    place = lax.axis_index("seq")
    first = place * length
    info = jnp.concatenate([doc_starts, jnp.stack([first, place % 2]).astype(jnp.int32)])

    block = pl.BlockSpec((BLK, width), lambda b, s: (b, 0))
    half_block = pl.BlockSpec((BLK, width // 2), lambda b, s: (b, 0))
    line = pl.BlockSpec((1, BLK), lambda b, s: (0, b))
    states = pl.BlockSpec((BLK // CHUNK, heads, HEAD_DIM, HEAD_DIM), lambda b, s: (b, 0, 0, 0))
    state = pl.BlockSpec((heads, HEAD_DIM, HEAD_DIM), lambda b, s: (0, 0, 0))
    one_state = shaped((heads, HEAD_DIM, HEAD_DIM), F32)
    low_state = shaped((heads, HEAD_DIM, HEAD_DIM), BF16)
    all_states = shaped((length // CHUNK, heads, HEAD_DIM, HEAD_DIM), F32)
    low_states = shaped((length // CHUNK, heads, HEAD_DIM, HEAD_DIM), BF16)
    tokens16 = shaped((length, width), BF16)
    tokens32 = shaped((length, width), F32)
    row = shaped((1, length), F32)
    scratch = [pltpu.VMEM((heads, HEAD_DIM, HEAD_DIM), F32)]

    kept = {}

    def early(landed):
        keys, values, _ = lax.optimization_barrier((key_rows, value_rows, landed))
        with jax.named_scope("key_states"):
            before, key_total = call(
                functools.partial(key_state_kernel, count, heads),
                "key_states",
                info,
                [keys, values],
                [block, block],
                [all_states, one_state],
                [states, state],
                scratch,
                12.0,
            )
        kept["before"] = before
        return key_total

    def middle(total, other, into, size):
        return combine(info, count, length, size, total, other, into)

    def late(product, into):
        kept["into"] = into
        tokens, _ = lax.optimization_barrier((queries, product))
        with jax.named_scope("attention"):
            kept["attn"], kept["square"], kept["low"] = call(
                functools.partial(attention_kernel, count, heads),
                "attention",
                info,
                [tokens, key_rows, value_rows, kept["before"], kept["into"]],
                [block, block, block, states, state],
                [tokens32, row, low_states],
                [block, line, states],
                (),
                8.0,
            )
        return kept["square"]

    near, far = grad_mixture(out_grad, out_weight, length, early, middle, late)
    attn, square, low = kept["attn"], kept["square"], kept["low"]

    with jax.named_scope("cross"):
        sums = call(
            functools.partial(cross_kernel, heads),
            "cross",
            info,
            [near, far, gate_out, attn, square],
            [half_block, half_block, block, block, line],
            [shaped((2, length), F32)],
            [pl.BlockSpec((2, BLK), lambda b, s: (0, b))],
        )[0]

    sums = head_sum(sums)

    back = lambda spec_shape, f: pl.BlockSpec(spec_shape, lambda b, s: f(nblocks - 1 - b))
    block_r = back((BLK, width), lambda b: (b, 0))
    half_r = back((BLK, width // 2), lambda b: (b, 0))
    line_r = back((2, BLK), lambda b: (0, b))
    states_r = back((BLK // CHUNK, heads, HEAD_DIM, HEAD_DIM), lambda b: (b, 0, 0, 0))
    with jax.named_scope("grad_attn"):
        grad, grad_gate, after, query_total, query_low = call(
            functools.partial(grad_attn_kernel, count, heads, full_width),
            "grad_attn",
            info,
            [near, far, gate_out, attn, queries, sums],
            [half_r, half_r, block_r, block_r, block_r, line_r],
            [tokens16, tokens16, all_states, one_state, low_state],
            [block_r, block_r, states_r, state, state],
            scratch,
            4.0,
        )
    landed = [
        flip(query_total if step == 1 else query_low, "seq", step)
        for step in range(1, lax.axis_size("seq"))
    ]
    big = pl.BlockSpec((LARGE, width), lambda b, s: (b, 0))
    big_states = pl.BlockSpec(
        (LARGE // CHUNK, heads, HEAD_DIM, HEAD_DIM), lambda b, s: (b, 0, 0, 0)
    )
    with jax.named_scope("grad_queries"):
        grad_queries = call(
            functools.partial(grad_query_kernel, count, heads),
            "grad_queries",
            info,
            [grad, key_rows, value_rows, low],
            [big, big, big, big_states],
            [tokens16],
            [big],
            (),
            8.0,
            LARGE,
        )[0]
    with jax.named_scope("grad_keys_values"):
        grad_keys, grad_values = call(
            functools.partial(grad_key_value_kernel, count, heads, length),
            "grad_keys_values",
            info,
            [grad, queries, key_rows, value_rows, after, *landed],
            [big, big, big, big, big_states] + [state] * len(landed),
            [tokens16, tokens16],
            [big, big],
            scratch,
            8.0,
            LARGE,
        )
    return (grad_queries, grad_keys, grad_values, grad_gate)


def solution(mesh):
    return jax.shard_map(
        body,
        mesh=mesh,
        in_specs=(
            P(("seq", "head"), None),
            P("head", None),
            P("seq", "head"),
            P("seq", "head"),
            P("seq", "head"),
            P("seq", "head"),
            P(),
        ),
        out_specs=(P("seq", "head"), P("seq", "head"), P("seq", "head"), P("seq", "head")),
        check_vma=False,
    )
```
